128 devices in a mesh: rotor: 8 (over y, core), stator: 16 (over x, z).
Axes of the slice: x: 4, y: 4, z: 4, core: 2. Of those that a mesh axis runs over, the one named last changes fastest.
Arguments:
- rotor_state: float32 [5, 8, 8, 8, 49152], P(None, None, None, None, ('rotor', 'stator')), as said below
- stator_state: float32 [5, 8, 8, 8, 49152], P(None, None, None, None, ('rotor', 'stator')), as said below
- rotor_projection: float32 [2, 64, 64], replicated, as said below
- proj_stator: float32 [2, 64, 64], replicated, as said below
- seg_owner: int32 [98304, 1], P(('rotor', 'stator')), may hold values from 0 to 127; in each aligned block of 768 rows (0 to 767, 768 to 1535, ...) at most 12 rows name the same one
- seg_row: int32 [98304], P(('rotor', 'stator')), may hold values from 0 to 383
Outputs:
- rotor_next: float32 [5, 8, 8, 8, 49152], P(None, None, None, None, ('rotor', 'stator'))
- stator_next: float32 [5, 8, 8, 8, 49152], P(None, None, None, None, ('rotor', 'stator'))
The draws below stay inside these ranges and needn't reach their ends.
Inputs may be any that keep to these rules, and one draw needn't show every extreme that they name: `seg_owner`: in each aligned block of 768 rows (the segments of one band device) no owner is named by more than 12 rows, a bound that some block reaches. `rotor_state`: density is positive at every node, and so is 0.4 (energy - |momentum|^2 / (2 density)). `stator_state`: density is positive at every node, and so is 0.4 (energy - |momentum|^2 / (2 density)). `rotor_projection`: entries are non-negative. `proj_stator`: entries are non-negative.
All inputs are finite; a program needn't handle non-finite values.
Results may differ from the reference program's by a relative error of at most 0.0001.
Values sent between devices are 32-bit elements; how exact they have to be, the bound alone decides.
A program may use at most 192 MiB of HBM per device.

```python
import math
import jax
import jax.numpy as jnp
import numpy as np
from jax import lax

NODES = 8
E_DEV = 384
INTERFACE_ELEMS = 49152
SEG_DEV = 768
SEGS = 98304
CAP = 12
N_ROTOR = 8
N_STATOR = 16
DEVICES = 128


GAMMA = 1.4


def conserved_draw(key, lower_bound, upper_bound, velocity_cap):
    subkeys = jax.random.split(key, 3)
    grid_shape = (NODES, NODES, NODES, INTERFACE_ELEMS)
    density = jnp.exp(jax.random.uniform(subkeys[0], grid_shape, jnp.float32, math.log(lower_bound), math.log(upper_bound)))
    velocity = jax.random.uniform(subkeys[1], (3,) + grid_shape, jnp.float32, -velocity_cap, velocity_cap)
    pressure = jnp.exp(jax.random.uniform(subkeys[2], grid_shape, jnp.float32, math.log(lower_bound), math.log(upper_bound)))
    momentum = density[None] * velocity
    energy = pressure / (GAMMA - 1.0) + 0.5 * density * jnp.sum(velocity * velocity, axis=0)
    return jnp.concatenate([density[None], momentum, energy[None]], axis=0)


def projection_draw(key, diagonal, spread):
    count = NODES * NODES
    random_part = jax.random.uniform(key, (2, count, count), jnp.float32, 0.0, spread)
    identity = jnp.eye(count, dtype=jnp.float32)
    return diagonal * identity[None] + random_part / count


def draw_rotor_state(key, part):
    key = jax.random.fold_in(key, 1)
    return conserved_draw(key, 0.5, 2.0, 0.6)


def draw_stator_state(key, part):
    key = jax.random.fold_in(key, 2)
    return conserved_draw(key, 0.5, 2.0, 0.6)


def draw_rotor_projection(key, part):
    key = jax.random.fold_in(key, 3)
    return projection_draw(key, 0.5, 1.0)


def draw_proj_stator(key, part):
    key = jax.random.fold_in(key, 4)
    return projection_draw(key, 0.5, 1.0)


def place_ends(drawn, rng, low, top_value):
    longest = drawn.shape.index(max(drawn.shape))
    spots = []
    for shift in (0, 1):
        where = [jax.random.randint(jax.random.fold_in(rng, axis), (), 0, length) for axis, length in enumerate(drawn.shape)]
        where[longest] = (where[longest] + shift) % drawn.shape[longest]
        spots.append(tuple(where))
    return drawn.at[spots[0]].set(low).at[spots[1]].set(top_value)


def shared_out(stream_key, own, number, rows, number_of, top, bound, slope):
    ranking = jax.random.permutation(stream_key, number_of)
    crowded, common = portions_of(number_of, rows * top, bound, slope, True), portions_of(number_of, rows * top, bound, slope, False)
    places = jnp.arange(number_of)

    def named(lengths, offset_by):
        used = int((lengths > 0).sum())
        fixed = max(1, used // 4)
        shifted = fixed + (places - fixed + offset_by * (used - fixed)) % max(1, number_of - fixed)
        return jnp.zeros((number_of,), jnp.int32).at[ranking[jnp.where(places < fixed, places, shifted)]].set(jnp.asarray(lengths, jnp.int32))

    lengths = jnp.where(number % 4 == 0, named(crowded, number // 4), named(common, number - number // 4 - 1))
    mixed = jax.random.permutation(jax.random.fold_in(own, 3), number_of)
    giver, taker = mixed[0:number_of // 2 * 2:2], mixed[1:number_of // 2 * 2:2]
    slack = jnp.minimum(lengths[giver] - 1, bound - lengths[taker]) // 2
    slack = jnp.where((giver == ranking[0]) | (taker == ranking[0]) | (lengths[taker] == 0), 0, jnp.maximum(slack, 0))
    shifted = jax.random.randint(jax.random.fold_in(own, 4), (number_of // 2,), 0, 1 << 20) % (slack + 1)
    lengths = lengths.at[giver].add(-shifted).at[taker].add(shifted)
    labels = jnp.searchsorted(jnp.cumsum(lengths), jnp.arange(rows * top), side="right").astype(jnp.int32)
    grid = labels.reshape(top, rows).T
    grid = grid[jax.random.permutation(jax.random.fold_in(own, 1), rows)]
    offset_by = jax.random.randint(jax.random.fold_in(own, 2), (rows, 1), 0, top)
    return jnp.take_along_axis(grid, (jnp.arange(top)[None, :] + offset_by) % top, axis=1)


def portions_of(number_of, total, limit, skew, full):
    weights = [(1 << 20) // math.isqrt(grade ** skew) + 1 for grade in range(1, number_of + 1)]
    largest = limit if full else min(limit, max(-(-total // number_of), total * weights[0] // sum(weights)))
    least = 1 if total - largest >= number_of - 1 else 0
    counts, rest = [largest] + [least] * (number_of - 1), total - largest - least * (number_of - 1)
    while rest > 0:
        candidates = [i for i in range(1, number_of) if counts[i] < largest] or [i for i in range(1, number_of) if counts[i] < limit]
        pool, left = sum([weights[i] for i in candidates]), rest
        for i in candidates:
            addition = min(limit - counts[i], max(1, left * weights[i] // pool), rest)
            counts[i] = counts[i] + addition
            rest = rest - addition
    return np.array(counts)


def setup_inputs(seed: int = 0) -> dict:
    streams_of = jax.random.split(jax.random.key(seed), 7)
    rotor_state = draw_rotor_state(jax.random.fold_in(streams_of[6], 71), 0)
    stator_state = draw_stator_state(jax.random.fold_in(streams_of[6], 71), 0)
    rotor_projection = draw_rotor_projection(jax.random.fold_in(streams_of[6], 71), 0)
    proj_stator = draw_proj_stator(jax.random.fold_in(streams_of[6], 71), 0)
    seg_owner_keys = jax.random.split(jax.random.fold_in(streams_of[4], 1), SEGS // SEG_DEV)
    seg_owner_turns = jax.random.permutation(jax.random.fold_in(streams_of[4], 3), SEGS // SEG_DEV)
    seg_owner = jax.vmap(lambda own, number: shared_out(jax.random.fold_in(streams_of[4], 2), own, number, SEG_DEV, DEVICES, 1, CAP, 2))(seg_owner_keys, seg_owner_turns).reshape((SEGS, 1))
    seg_row = place_ends(jax.random.randint(streams_of[5], (SEGS,), 0, E_DEV), jax.random.fold_in(streams_of[5], 1), 0, E_DEV - 1).astype(jnp.int32)
    return {"rotor_state": rotor_state, "stator_state": stator_state, "rotor_projection": rotor_projection, "proj_stator": proj_stator, "seg_owner": seg_owner, "seg_row": seg_row}


GAMMA = 1.4
TIME_STEP = 0.02
LIFT_FACTOR = 28.0
TOP_PRECISION = lax.Precision.HIGHEST

def cheb_matrix():
    degree = NODES - 1
    j = np.arange(degree + 1)
    points = -np.cos(np.pi * j / degree)
    weights = np.where((j == 0) | (j == degree), 2.0, 1.0) * (-1.0) ** j
    spacing = points[:, None] - points[None, :]
    identity = np.eye(degree + 1)
    matrix = weights[:, None] / weights[None, :] / (spacing + identity)
    matrix = matrix - identity * matrix.sum(axis=1)[:, None]
    return matrix.astype(np.float32)

def primitive(fields):
    density, momentum_x, momentum_y, momentum_z, energy = fields
    inverse = 1.0 / density
    velocity = (momentum_x * inverse, momentum_y * inverse, momentum_z * inverse)
    kinetic = momentum_x * velocity[0] + momentum_y * velocity[1] + momentum_z * velocity[2]
    pressure = (GAMMA - 1.0) * (energy - 0.5 * kinetic)
    return (velocity, pressure)

def directional_flux(fields, velocity, pressure, direction):
    normal_speed = velocity[direction]
    result = [fields[1 + direction]]
    for component in range(3):
        product = fields[1 + component] * normal_speed
        if component == direction:
            product = product + pressure
        result.append(product)
    result.append((fields[4] + pressure) * normal_speed)
    return result

def rusanov(rotor_side, stator_side):
    left_fields = [rotor_side[..., variable, :] for variable in range(5)]
    right_fields = [stator_side[..., variable, :] for variable in range(5)]
    left_velocity, left_pressure = primitive(left_fields)
    right_velocity, right_pressure = primitive(right_fields)
    left_flux = directional_flux(left_fields, left_velocity, left_pressure, 2)
    right_flux = directional_flux(right_fields, right_velocity, right_pressure, 2)
    signal = jnp.maximum(jnp.abs(left_velocity[2]) + jnp.sqrt(GAMMA * left_pressure / left_fields[0]), jnp.abs(right_velocity[2]) + jnp.sqrt(GAMMA * right_pressure / right_fields[0]))
    merged = [0.5 * (left_flux[variable] + right_flux[variable]) - 0.5 * signal * (right_fields[variable] - left_fields[variable]) for variable in range(5)]
    return jnp.stack(merged, axis=-2)

def volume_rate(conserved, matrix):
    fields = [conserved[variable] for variable in range(5)]
    velocity, pressure = primitive(fields)
    patterns = ('ij,vjbce->vibce', 'ij,vajce->vaice', 'ij,vabje->vabie')
    divergence = jnp.zeros_like(conserved)
    for direction in range(3):
        flux_values = jnp.stack(directional_flux(fields, velocity, pressure, direction))
        divergence = divergence + jnp.einsum(patterns[direction], matrix, flux_values, precision=TOP_PRECISION)
    return -divergence

def face_flux(face_state):
    fields = [face_state[variable] for variable in range(5)]
    velocity, pressure = primitive(fields)
    return jnp.stack(directional_flux(fields, velocity, pressure, 2))

def project_select(matrices, traces, side_bit):
    projected = jnp.einsum('sij,...vj->...svi', matrices, traces, precision=TOP_PRECISION)
    return jnp.where((side_bit == 0)[..., None, None], projected[..., 0, :, :], projected[..., 1, :, :])

def adjoint_select(matrices, flux_values, side_bit):
    projected = jnp.einsum('sji,...vj->...svi', matrices, flux_values, precision=TOP_PRECISION)
    return 0.5 * jnp.where((side_bit == 0)[..., None, None], projected[..., 0, :, :], projected[..., 1, :, :])

def blockwise(conserved, matrix):
    blocks = jnp.moveaxis(conserved.reshape(5, NODES, NODES, NODES, DEVICES, E_DEV), 4, 0)
    rates = lax.map(lambda piece: volume_rate(piece, matrix), blocks)
    return jnp.moveaxis(rates, 0, 4).reshape(conserved.shape)

def reference(rotor_state, stator_state, rotor_projection, proj_stator, seg_owner, seg_row):
    matrix = jnp.asarray(cheb_matrix())
    rotor_rate = blockwise(rotor_state, matrix)
    stator_rate = blockwise(stator_state, matrix)
    band_block = E_DEV // N_ROTOR
    surface_nodes = NODES * NODES
    rotor_face = rotor_state[:, :, :, NODES - 1, :].reshape(5, surface_nodes, N_ROTOR, N_STATOR, N_ROTOR, band_block)
    banded = rotor_face.transpose(0, 1, 4, 3, 2, 5).reshape(5, surface_nodes, INTERFACE_ELEMS)
    rotor_side = jnp.einsum('sij,vjf->fsvi', rotor_projection, banded, precision=TOP_PRECISION).reshape(SEGS, 5, surface_nodes)
    stator_rows = stator_state[:, :, :, 0, :].reshape(5, surface_nodes, INTERFACE_ELEMS).transpose(2, 0, 1)
    target = seg_owner[:, 0] * E_DEV + seg_row
    side_bit = jnp.arange(SEGS, dtype=jnp.int32) % 2
    stator_side = project_select(proj_stator, stator_rows[target], side_bit)
    flux_values = rusanov(rotor_side, stator_side)
    rotor_face_flux = 0.5 * jnp.einsum('glo,qgxl->xoq', rotor_projection, flux_values.reshape(INTERFACE_ELEMS, 2, 5, surface_nodes), precision=TOP_PRECISION)
    rotor_face_flux = rotor_face_flux.reshape(5, surface_nodes, N_ROTOR, N_STATOR, N_ROTOR, band_block).transpose(0, 1, 4, 3, 2, 5)
    rotor_face_flux = rotor_face_flux.reshape(5, NODES, NODES, INTERFACE_ELEMS)
    stator_part = adjoint_select(proj_stator, flux_values, side_bit)
    stator_flux = jax.ops.segment_sum(stator_part.reshape(SEGS, 5 * surface_nodes), target, num_segments=INTERFACE_ELEMS)
    stator_flux = stator_flux.T.reshape(5, NODES, NODES, INTERFACE_ELEMS)
    rotor_rate = rotor_rate.at[:, :, :, NODES - 1, :].add(-LIFT_FACTOR * (rotor_face_flux - face_flux(rotor_state[:, :, :, NODES - 1, :])))
    stator_rate = stator_rate.at[:, :, :, 0, :].add(LIFT_FACTOR * (stator_flux - face_flux(stator_state[:, :, :, 0, :])))
    return (rotor_state + TIME_STEP * rotor_rate, stator_state + TIME_STEP * stator_rate)
```

```python
import functools

import jax
import jax.numpy as jnp
import numpy as np
from jax import lax
from jax.experimental import pallas as pl
from jax.experimental.pallas import tpu as pltpu
from jax.sharding import PartitionSpec as P

NODES = 8
FACE = 64
NR = 8
NS = 16
ND = NR * NS
ELEMS = 384
BAND = ELEMS // NR
SEGS = 2 * ELEMS
ROWS = 5 * NODES * FACE
CAP = 12
PAIRS = CAP // 2
HALF = PAIRS // 2
MSG = 16
CHUNK_ROWS = ND * MSG
WIDE = 5 * 128
GAMMA = 1.4
TIME_STEP = 0.02
LIFT = 28.0
MESH = pl.DeviceIdType.MESH
F32 = jnp.float32
BF16 = jnp.bfloat16


def cheb_matrix():
    degree = NODES - 1
    j = np.arange(degree + 1)
    points = -np.cos(np.pi * j / degree)
    weights = np.where((j == 0) | (j == degree), 2.0, 1.0) * (-1.0) ** j
    spacing = points[:, None] - points[None, :]
    identity = np.eye(degree + 1)
    matrix = weights[:, None] / weights[None, :] / (spacing + identity)
    matrix = matrix - identity * matrix.sum(axis=1)[:, None]
    return matrix.astype(np.float32)


DM = cheb_matrix().astype(np.float64) * (-TIME_STEP * 0.5)
ODD = DM[:4, :4] - DM[:4, :3:-1]
EVEN = DM[:4, :4] + DM[:4, :3:-1]


def derive(line):
    plus = [line[j] + line[7 - j] for j in range(4)]
    minus = [line[j] - line[7 - j] for j in range(4)]
    out = [None] * 8
    for i in range(4):
        p = sum(float(ODD[i, j]) * minus[j] for j in range(4))
        q = sum(float(EVEN[i, j]) * plus[j] for j in range(4))
        out[i] = p + q
        out[7 - i] = p - q
    return out


def primitive(fields):
    density, mx, my, mz, energy = fields
    inverse = 1.0 / density
    u = (mx * inverse, my * inverse, mz * inverse)
    kinetic = mx * u[0] + my * u[1] + mz * u[2]
    return u, (GAMMA - 1.0) * (energy - 0.5 * kinetic), inverse


def flux_along(fields, speed, pressure, direction):
    result = [fields[1 + direction]]
    for k in range(3):
        term = fields[1 + k] * speed
        result.append(term + pressure if k == direction else term)
    result.append((fields[4] + pressure) * speed)
    return result


def rusanov(left, right):
    lu, lp, li = primitive(left)
    ru, rp, ri = primitive(right)
    lf = flux_along(left, lu[2], lp, 2)
    rf = flux_along(right, ru[2], rp, 2)
    signal = jnp.maximum(
        jnp.abs(lu[2]) + jnp.sqrt(GAMMA * lp * li), jnp.abs(ru[2]) + jnp.sqrt(GAMMA * rp * ri)
    )
    return [
        0.5 * (lf[v] + rf[v]) - 0.5 * signal * (right[v] - left[v]) for v in range(5)
    ]


def split(x):
    hi = x.astype(BF16)
    return hi, (x - hi.astype(F32)).astype(BF16)


def dot_nn(a, b):
    return lax.dot_general(a, b, (((1,), (0,)), ((), ())), preferred_element_type=F32)


def dot_nt(a, b):
    return lax.dot_general(a, b, (((1,), (1,)), ((), ())), preferred_element_type=F32)


def dot3(dot, a, b):
    return dot(a[0], b[0]) + dot(a[0], b[1]) + dot(a[1], b[0])


def hot(mask):
    return jnp.where(mask, 1.0, 0.0).astype(BF16)


def iota(shape, dim):
    return lax.broadcasted_iota(jnp.int32, shape, dim)


def volume_first(src, prim, tmp, acc, step):
    t, a = lax.div(step, 8), lax.rem(step, 8)
    at = lambda v, b: pl.ds(pl.multiple_of(v * 512 + a * 64 + b * 8, 8), 8)
    lines = [[] for _ in range(5)]
    for b in range(8):
        fields = [src[t, at(v, b), :] for v in range(5)]
        u, p, _ = primitive(fields)
        prim[at(0, b), :] = u[0]
        prim[at(1, b), :] = u[2]
        prim[at(2, b), :] = p
        for v, value in enumerate(flux_along(fields, u[1], p, 1)):
            lines[v].append(value)
    for v in range(5):
        for b, value in enumerate(derive(lines[v])):
            acc[at(v, b), :] = value
    column = lambda v, c: pl.ds(v * 512 + a * 64 + c, 8, stride=8)
    lines = [[] for _ in range(5)]
    for c in range(8):
        fields = [None] + [src[t, column(v, c), :] for v in range(1, 5)]
        for v, value in enumerate(
            flux_along(fields, prim[column(1, c), :], prim[column(2, c), :], 2)
        ):
            lines[v].append(value)
    for v in range(5):
        for c, value in enumerate(derive(lines[v])):
            tmp[pl.ds(v * 64 + c, 8, stride=8), :] = value
    for v in range(5):
        for b in range(8):
            acc[at(v, b), :] += tmp[v * 64 + b * 8 : v * 64 + b * 8 + 8, :]


def volume_second(src, prim, acc, out, t, b):
    at = lambda v, a: pl.ds(pl.multiple_of(v * 512 + a * 64 + b * 8, 8), 8)
    lines = [[] for _ in range(5)]
    for a in range(8):
        fields = [None] + [src[t, at(v, a), :] for v in range(1, 5)]
        for v, value in enumerate(
            flux_along(fields, prim[at(0, a), :], prim[at(2, a), :], 0)
        ):
            lines[v].append(value)
    for v in range(5):
        for a, value in enumerate(derive(lines[v])):
            out[t, at(v, a), :] = src[t, at(v, a), :] + (acc[at(v, a), :] + value)


def volume(src, out, prim, tmp, acc, tiles):
    for t in tiles:

        def first(a, carry):
            volume_first(src, prim, tmp, acc, t * 8 + a)
            return carry

        def second(b, carry):
            volume_second(src, prim, acc, out, t, b)
            return carry

        lax.fori_loop(0, 8, first, 0)
        lax.fori_loop(0, 8, second, 0)


def face_rows(src, node, dst):
    for t in range(3):
        count = 128 if t < 2 else 64
        rows = [
            src[g, pl.ds(t * 1024 + node, count, stride=8), :]
            for g in range(3)
        ]
        for g in range(3):
            block = rows[g]
            if t == 2:
                block = jnp.concatenate([block, jnp.zeros((64, 128), F32)], axis=0)
            dst[g * 128 : g * 128 + 128, t * 128 : t * 128 + 128] = block.T


def place(matrix, half):
    zero = jnp.zeros((FACE, FACE), F32)
    return jnp.concatenate([matrix, zero] if half == 0 else [zero, matrix], axis=1)


def make_table(faces, proj, hi_ref, lo_ref, side_ref):
    zero = jnp.zeros((FACE, 128), F32)
    lower = iota((128, 128), 1) < FACE
    for s in range(2):
        kept = []
        for vh in range(2):
            block = place(proj[s], vh)
            for par in range(2):
                kept.append(jnp.concatenate([block, zero] if par == 0 else [zero, block], axis=0))
        weights = split(jnp.concatenate(kept, axis=0))
        for t in range(3):
            count = 512 if t < 2 else 256
            w = (weights[0][:count], weights[1][:count])

            def body(g, carry):
                rows = pl.ds(pl.multiple_of(g * 128, 128), 128)
                x = split(faces[rows, t * 128 : t * 128 + 128])
                y = dot3(dot_nt, x, w)
                for vh in range(count // 256):
                    v = 2 * t + vh
                    for par in range(2):
                        piece = y[:, (vh * 2 + par) * 128 : (vh * 2 + par + 1) * 128]
                        hi, lo = split(piece)
                        dst = pl.ds(pl.multiple_of((par * 2 + s) * ELEMS + g * 128, 128), 128)
                        hi_ref[dst, v * 128 : v * 128 + 128] = hi
                        lo_ref[dst, v * 128 : v * 128 + 128] = lo
                        if side_ref is not None and par == s:
                            if s == 0:
                                side_ref[rows, v * 128 : v * 128 + 128] = piece
                            else:
                                side_ref[rows, v * 128 : v * 128 + 128] += piece
                return carry

            lax.fori_loop(0, 3, body, 0)


def gather_chunk(chunk, hots, hi_ref, lo_ref, message):
    x = hots[...]
    for v in range(5):
        cols = slice(v * 128, v * 128 + 128)
        y = dot_nn(x, hi_ref[:, cols]) + dot_nn(x, lo_ref[:, cols])
        for pp in range(HALF):
            message[pl.ds(chunk * CHUNK_ROWS + v * HALF + pp, ND, stride=MSG), :] = y[
                pp * ND : pp * ND + ND, :
            ]


def mega(
    owner_ref, row_ref, rproj_ref, sproj_ref, rstate, sstate,
    rvol, svol, rsurf, ssurf,
    rs, ss, ru, su, prim, tmp, acc,
    faces_s, faces_r, bands, code_out, code_in, codes, seg,
    tab_hi, tab_lo, ltab_hi, ltab_lo, lside, rside, hots,
    rout, rin, lout, lin, rflux, rflux_in, fluxes_hi, fluxes_lo, sums,
    load_sem, store_sem, own_sem, code_sem, trace_sem, send_sem, r_sem, l_sem, back_sem,
):
    mi, mj = lax.axis_index("rotor"), lax.axis_index("stator")
    me = mi * NS + mj
    tiles = lambda ref, t: ref.at[:, pl.ds(t * 128, 128)]
    loads = [
        [
            pltpu.make_async_copy(tiles(state, t), held.at[t], load_sem.at[n, t])
            for t in range(3)
        ]
        for n, (state, held) in enumerate(((rstate, rs), (sstate, ss)))
    ]
    for copy in loads[0] + loads[1]:
        copy.start()

    def coords(d):
        return (lax.div(d, NS), lax.rem(d, NS))

    def peer(p):
        q = 1 + lax.rem(p + me * 55, ND - 1)
        o = lax.rem(q * 37, ND)
        i = lax.rem(lax.div(o, NS) + mi, NR)
        j = lax.rem(lax.rem(o, NS) + mj, NS)
        return i, j

    barrier = pltpu.get_barrier_semaphore()

    def greet(p, carry):
        pl.semaphore_signal(
            barrier, inc=1, device_id=coords(lax.rem(me + p, ND)), device_id_type=MESH
        )
        return carry

    lax.fori_loop(1, ND, greet, 0)

    owner = owner_ref[...].astype(F32)
    code = row_ref[...]
    lane = iota((1, SEGS), 1)
    side = lax.rem(lane, 2)
    code = code + side * ELEMS + 1
    high = lax.div(code, 4).astype(F32)
    low = lax.rem(code, 4).astype(F32)
    packed = jnp.concatenate([owner, high, low, jnp.zeros((5, SEGS), F32)], axis=0).astype(BF16)
    new = iota((SEGS, SEGS), 0)
    old = iota((SEGS, SEGS), 1)
    order = hot(old == jnp.where(new < ELEMS, 2 * new, 2 * new - 2 * ELEMS + 1))
    by_side = dot_nt(packed, order)
    owner = by_side[0:1]
    member = owner == iota((ND, SEGS), 0).astype(F32)
    member_hot = hot(member)
    earlier = dot_nn(member_hot, hot(new < old))
    rank = jnp.sum(jnp.where(member, earlier, 0.0), axis=0, keepdims=True)
    seg[0:1, :] = owner
    seg[1:2, :] = rank
    seg[2:8, :] = jnp.zeros((6, SEGS), F32)
    ranked = rank == iota((ND, SEGS), 0).astype(F32)
    table = 4.0 * dot_nt(member_hot, jnp.where(ranked, by_side[1:2], 0.0).astype(BF16))
    table = table + dot_nt(member_hot, jnp.where(ranked, by_side[2:3], 0.0).astype(BF16))
    code_out[...] = table.reshape(ND, 1, 128)

    for copy in loads[0]:
        copy.wait()
    face_rows(rs, NODES - 1, faces_r)
    for copy in loads[1]:
        copy.wait()
    face_rows(ss, 0, faces_s)
    make_table(faces_s, sproj_ref, tab_hi, tab_lo, None)
    volume(rs, ru, prim, tmp, acc, range(3))

    pl.semaphore_wait(barrier, ND - 1)

    def send_code(p, carry):
        i, j = peer(p)
        pltpu.make_async_remote_copy(
            src_ref=code_out.at[i * NS + j], dst_ref=code_in.at[me],
            send_sem=code_sem.at[0], recv_sem=code_sem.at[1],
            device_id=(i, j), device_id_type=MESH,
        ).start()
        return carry

    lax.fori_loop(0, ND - 1, send_code, 0)

    def ring(src, dst, sems, me_rows):
        def send(p, carry):
            i = lax.rem(mi + p, NR)
            pltpu.make_async_remote_copy(
                src_ref=src.at[pl.ds(pl.multiple_of(i * BAND, 16), BAND)],
                dst_ref=dst.at[me_rows],
                send_sem=sems.at[0], recv_sem=sems.at[1],
                device_id=(i, mj), device_id_type=MESH,
            ).start()
            return carry

        lax.fori_loop(1, NR, send, 0)

    def ring_wait(dst, sem):
        rows = dst.at[pl.ds(0, (NR - 1) * BAND)]
        pltpu.make_async_copy(rows, rows, sem).wait()

    my_rows = pl.ds(pl.multiple_of(mi * BAND, 16), BAND)
    ring(faces_r, bands, trace_sem, my_rows)
    own = pltpu.make_async_copy(code_out.at[me], code_in.at[me], own_sem.at[0])
    own.start()
    own_trace = pltpu.make_async_copy(faces_r.at[my_rows], bands.at[my_rows], own_sem.at[1])
    own_trace.start()

    volume(ss, su, prim, tmp, acc, range(1))

    own.wait()
    part = code_in.at[pl.ds(0, ND - 1)]
    pltpu.make_async_copy(part, part, code_sem.at[1]).wait()
    codes[...] = code_in[...].reshape(ND, 128)

    def send_chunk(chunk, src, dst, sems):
        def send(p, carry):
            i, j = peer(p)
            at = pl.ds(pl.multiple_of(chunk * CHUNK_ROWS + (i * NS + j) * MSG, MSG), MSG)
            to = pl.ds(pl.multiple_of(chunk * CHUNK_ROWS + me * MSG, MSG), MSG)
            pltpu.make_async_remote_copy(
                src_ref=src.at[at], dst_ref=dst.at[to],
                send_sem=send_sem, recv_sem=sems.at[chunk],
                device_id=(i, j), device_id_type=MESH,
            ).start()
            return carry

        lax.fori_loop(0, ND - 1, send, 0)

    def wait_chunk(chunk, dst, sems):
        rows = dst.at[pl.ds(chunk * CHUNK_ROWS, (ND - 1) * MSG)]
        pltpu.make_async_copy(rows, rows, sems.at[chunk]).wait()

    def own_chunk(chunk, src, dst, sem):
        to = pl.ds(pl.multiple_of(chunk * CHUNK_ROWS + me * MSG, MSG), MSG)
        return pltpu.make_async_copy(src.at[to], dst.at[to], sem)

    for chunk in range(2):
        for pp in range(HALF):
            for par in range(2):
                slot = 2 * (chunk * HALF + pp) + par
                column = codes[:, slot : slot + 1].astype(jnp.int32) - 1
                hots[pp * ND : pp * ND + ND, par * SEGS : par * SEGS + SEGS] = hot(
                    column == iota((ND, SEGS), 1)
                )
        gather_chunk(chunk, hots, tab_hi, tab_lo, rout)
        send_chunk(chunk, rout, rin, r_sem)
        own_chunk(chunk, rout, rin, own_sem.at[2 + chunk]).start()

    own_trace.wait()
    ring_wait(bands, trace_sem.at[1])
    make_table(bands, rproj_ref, ltab_hi, ltab_lo, lside)
    for chunk in range(2):
        belongs = seg[0:1, :] == iota((ND, SEGS), 0).astype(F32)
        for pp in range(HALF):
            for par in range(2):
                slot = 2 * (chunk * HALF + pp) + par
                hots[pp * ND : pp * ND + ND, par * SEGS : par * SEGS + SEGS] = hot(
                    jnp.logical_and(belongs, seg[1:2, :] == float(slot))
                )
        gather_chunk(chunk, hots, ltab_hi, ltab_lo, lout)
        send_chunk(chunk, lout, lin, l_sem)
        own_chunk(chunk, lout, lin, own_sem.at[4 + chunk]).start()

    volume(ss, su, prim, tmp, acc, range(1, 3))
    stores = [
        pltpu.make_async_copy(held.at[t], tiles(vol, t), store_sem.at[n, t])
        for n, (held, vol) in enumerate(((ru, rvol), (su, svol)))
        for t in range(3)
    ]
    for copy in stores:
        copy.start()

    columns = seg[...].T
    for chunk in range(2):
        own_chunk(chunk, rout, rin, own_sem.at[2 + chunk]).wait()
        wait_chunk(chunk, rin, r_sem)
        for pp in range(HALF):
            at = slice((chunk * HALF + pp) * ND, (chunk * HALF + pp + 1) * ND)
            for v in range(5):
                x = rin[pl.ds(chunk * CHUNK_ROWS + v * HALF + pp, ND, stride=MSG), :]
                hi, lo = split(x)
                fluxes_hi[at, v * 128 : v * 128 + 128] = hi
                fluxes_lo[at, v * 128 : v * 128 + 128] = lo
    lower = iota((ELEMS, 128), 1) < FACE
    for s in range(2):
        mine = columns[s * ELEMS : s * ELEMS + ELEMS, :]
        ranks = mine[:, 1:2].astype(jnp.int32)
        owners = mine[:, 0:1].astype(jnp.int32)
        picks = []
        for par in range(2):
            slot = jnp.where(lax.rem(ranks, 2) == par, lax.div(ranks, 2) * ND + owners, -1)
            picks.append(hot(slot == iota((ELEMS, SEGS), 1)))
        for v in range(5):
            cols = slice(v * 128, v * 128 + 128)
            hi, lo = fluxes_hi[:, cols], fluxes_lo[:, cols]
            y = [dot_nn(x, hi) + dot_nn(x, lo) for x in picks]
            y = jnp.where(lower, y[0], y[1])
            y = y + pltpu.roll(y, FACE, 1)
            if s == 0:
                rside[:, cols] = y
            else:
                rside[:, cols] = jnp.where(lower, rside[:, cols], y)
    both = [rproj_ref[0], rproj_ref[1]]
    back = [
        split(jnp.concatenate([place(m, half) for m in both], axis=0)) for half in range(2)
    ]

    def band_flux(g, carry):
        rows = pl.ds(pl.multiple_of(g * 128, 128), 128)
        left = [lside[rows, v * 128 : v * 128 + 128] for v in range(5)]
        right = [rside[rows, v * 128 : v * 128 + 128] for v in range(5)]
        flux = [split(x) for x in rusanov(left, right)]
        for t in range(3):
            y = dot3(dot_nn, flux[2 * t], back[0])
            if t < 2:
                y = y + dot3(dot_nn, flux[2 * t + 1], back[1])
            rflux[rows, t * 128 : t * 128 + 128] = y
        return carry

    lax.fori_loop(0, 3, band_flux, 0)
    ring(rflux, rflux_in, back_sem, my_rows)
    own_back = pltpu.make_async_copy(rflux.at[my_rows], rflux_in.at[my_rows], own_sem.at[6])
    own_back.start()

    code_rows = codes[...].T
    for chunk in range(2):
        own_chunk(chunk, lout, lin, own_sem.at[4 + chunk]).wait()
        wait_chunk(chunk, lin, l_sem)
        for pp in range(HALF):
            at = lambda v: pl.ds(chunk * CHUNK_ROWS + v * HALF + pp, ND, stride=MSG)
            slot = 2 * (chunk * HALF + pp)
            named = jnp.where(
                iota((ND, 128), 1) < FACE, codes[:, slot : slot + 1], codes[:, slot + 1 : slot + 2]
            )
            flux = rusanov([lin[at(v), :] for v in range(5)], [rout[at(v), :] for v in range(5)])
            for v in range(5):
                hi, lo = split(jnp.where(named > 0.5, flux[v], 0.0))
                fluxes_hi[pp * ND : pp * ND + ND, v * 128 : v * 128 + 128] = hi
                fluxes_lo[pp * ND : pp * ND + ND, v * 128 : v * 128 + 128] = lo
        for s in range(2):
            picks = []
            for par in range(2):
                pieces = []
                for pp in range(HALF):
                    slot = 2 * (chunk * HALF + pp) + par
                    line = code_rows[slot : slot + 1, :].astype(jnp.int32) - (1 + s * ELEMS)
                    pieces.append(hot(line == iota((ELEMS, ND), 0)))
                picks.append(jnp.concatenate(pieces, axis=1))
            for v in range(5):
                cols = slice(v * 128, v * 128 + 128)
                hi, lo = fluxes_hi[0 : HALF * ND, cols], fluxes_lo[0 : HALF * ND, cols]
                y = [dot_nn(x, hi) + dot_nn(x, lo) for x in picks]
                y = jnp.where(lower, y[0], y[1])
                rows = slice(s * ELEMS, s * ELEMS + ELEMS)
                if chunk == 0:
                    sums[rows, cols] = y
                else:
                    sums[rows, cols] += y

    def face_flux(src, node):
        at = lambda v: pl.ds(v * 512 + node, FACE, stride=8)
        result = [[] for _ in range(5)]
        for g in range(3):
            fields = [src[g, at(v), :] for v in range(5)]
            u, p, _ = primitive(fields)
            for v, value in enumerate(flux_along(fields, u[2], p, 2)):
                result[v].append(value)
        return [jnp.concatenate(r, axis=1) for r in result]

    adjoint = []
    for s in range(2):
        wide = jnp.concatenate([sproj_ref[s], jnp.zeros((FACE, FACE), F32)], axis=1)
        turned = jnp.concatenate([wide, wide], axis=0).T
        adjoint.append(split(turned[:FACE, :]))
    mine = face_flux(ss, 0)
    for v in range(5):
        cols = slice(v * 128, v * 128 + 128)
        y = dot3(dot_nt, adjoint[0], split(sums[0:ELEMS, cols]))
        y = y + dot3(dot_nt, adjoint[1], split(sums[ELEMS : 2 * ELEMS, cols]))
        ssurf[v * FACE : v * FACE + FACE, :] = (TIME_STEP * LIFT) * (0.5 * y - mine[v])

    own_back.wait()
    ring_wait(rflux_in, back_sem.at[1])
    mine = face_flux(rs, NODES - 1)
    for t in range(3):
        turned = jnp.concatenate(
            [rflux_in[g * 128 : g * 128 + 128, t * 128 : t * 128 + 128].T for g in range(3)], axis=1
        )
        for vh in range(2 if t < 2 else 1):
            v = 2 * t + vh
            y = turned[vh * FACE : vh * FACE + FACE, :]
            rsurf[v * FACE : v * FACE + FACE, :] = (-TIME_STEP * LIFT) * (0.5 * y - mine[v])

    for copy in stores:
        copy.wait()
    part = code_out.at[pl.ds(0, ND - 1)]
    pltpu.make_async_copy(part, part, code_sem.at[0]).wait()
    ring_wait(faces_r, trace_sem.at[0])
    ring_wait(rflux, back_sem.at[0])
    for chunk in range(4):
        rows = rout.at[pl.ds(0, (ND - 1) * MSG)]
        pltpu.make_async_copy(rows, rows, send_sem).wait()


def finish(rvol, svol, rsurf, ssurf, rnext, snext):
    for node, vol, surf, out in ((NODES - 1, rvol, rsurf, rnext), (0, svol, ssurf, snext)):
        at = pl.ds(node, FACE, stride=8)
        out[...] = vol[...]
        out[at, :] = vol[at, :] + surf[...]


def body(rotor_state, stator_state, rotor_projection, proj_stator, seg_owner, seg_row):
    vmem = pl.BlockSpec(memory_space=pltpu.VMEM)
    hbm = pl.BlockSpec(memory_space=pl.ANY)
    V = pltpu.VMEM
    dma = pltpu.SemaphoreType.DMA
    state = (ROWS, ELEMS)
    held = (3, ROWS, 128)
    big = jax.ShapeDtypeStruct(state, F32)
    small = jax.ShapeDtypeStruct((5 * FACE, ELEMS), F32)
    parts = pl.pallas_call(
        mega,
        out_shape=(big, big, small, small),
        in_specs=[vmem, vmem, vmem, vmem, hbm, hbm],
        out_specs=(hbm, hbm, vmem, vmem),
        scratch_shapes=[
            V(held, F32), V(held, F32), V(held, F32), V(held, F32),
            V((3 * 512, 128), F32), V((320, 128), F32), V((ROWS, 128), F32),
            V((ELEMS, 384), F32), V((ELEMS, 384), F32), V((ELEMS, 384), F32),
            V((ND, 1, 128), F32), V((ND, 1, 128), F32), V((ND, 128), F32), V((8, SEGS), F32),
            V((2 * SEGS, WIDE), BF16), V((2 * SEGS, WIDE), BF16),
            V((2 * SEGS, WIDE), BF16), V((2 * SEGS, WIDE), BF16),
            V((ELEMS, WIDE), F32), V((ELEMS, WIDE), F32), V((HALF * ND, 2 * SEGS), BF16),
            V((2 * CHUNK_ROWS, 128), F32), V((2 * CHUNK_ROWS, 128), F32),
            V((2 * CHUNK_ROWS, 128), F32), V((2 * CHUNK_ROWS, 128), F32),
            V((ELEMS, 384), F32), V((ELEMS, 384), F32),
            V((SEGS, WIDE), BF16), V((SEGS, WIDE), BF16), V((SEGS, WIDE), F32),
            dma((2, 3)), dma((2, 3)), dma((7,)), dma((2,)), dma((2,)), dma, dma((2,)), dma((2,)), dma((2,)),
        ],
        compiler_params=pltpu.CompilerParams(
            collective_id=0, has_side_effects=True, vmem_limit_bytes=56 * 2**20
        ),
    )(
        seg_owner.reshape(1, SEGS),
        seg_row.reshape(1, SEGS),
        rotor_projection,
        proj_stator,
        rotor_state.reshape(state),
        stator_state.reshape(state),
    )
    block = pl.BlockSpec((512, 128), lambda v, g: (v, g))
    face = pl.BlockSpec((FACE, 128), lambda v, g: (v, g))
    rotor_next, stator_next = pl.pallas_call(
        finish,
        grid=(5, 3),
        out_shape=(big, big),
        in_specs=[block, block, face, face],
        out_specs=(block, block),
        compiler_params=pltpu.CompilerParams(vmem_limit_bytes=32 * 2**20),
    )(*parts)
    return rotor_next.reshape(rotor_state.shape), stator_next.reshape(stator_state.shape)


def solution(mesh):
    spec = P(None, None, None, None, ("rotor", "stator"))
    in_specs = (spec, spec, P(), P(), P(("rotor", "stator"), None), P(("rotor", "stator")))
    return jax.shard_map(body, mesh=mesh, in_specs=in_specs, out_specs=(spec, spec), check_vma=False)
```

```python
import functools

import jax
import jax.numpy as jnp
import numpy as np
from jax import lax
from jax.experimental import pallas as pl
from jax.experimental.pallas import tpu as pltpu
from jax.sharding import PartitionSpec as P

NODES = 8
FACE = 64
NR = 8
NS = 16
ND = NR * NS
ELEMS = 384
BAND = ELEMS // NR
SEGS = 2 * ELEMS
ROWS = 5 * NODES * FACE
CAP = 12
PAIRS = CAP // 2
HALF = PAIRS // 2
MSG = 16
SENT = 15
CHUNK_ROWS = ND * MSG
WIDE = 5 * 128
GAMMA = 1.4
TIME_STEP = 0.02
LIFT = 28.0
MESH = pl.DeviceIdType.MESH
F32 = jnp.float32
BF16 = jnp.bfloat16


def cheb_matrix():
    degree = NODES - 1
    j = np.arange(degree + 1)
    points = -np.cos(np.pi * j / degree)
    weights = np.where((j == 0) | (j == degree), 2.0, 1.0) * (-1.0) ** j
    spacing = points[:, None] - points[None, :]
    identity = np.eye(degree + 1)
    matrix = weights[:, None] / weights[None, :] / (spacing + identity)
    matrix = matrix - identity * matrix.sum(axis=1)[:, None]
    return matrix.astype(np.float32)


DM = cheb_matrix().astype(np.float64) * (-TIME_STEP * 0.5)
ODD = DM[:4, :4] - DM[:4, :3:-1]
EVEN = DM[:4, :4] + DM[:4, :3:-1]


def derive(line):
    plus = [line[j] + line[7 - j] for j in range(4)]
    minus = [line[j] - line[7 - j] for j in range(4)]
    out = [None] * 8
    for i in range(4):
        p = sum(float(ODD[i, j]) * minus[j] for j in range(4))
        q = sum(float(EVEN[i, j]) * plus[j] for j in range(4))
        out[i] = p + q
        out[7 - i] = p - q
    return out


def primitive(fields):
    density, mx, my, mz, energy = fields
    inverse = 1.0 / density
    u = (mx * inverse, my * inverse, mz * inverse)
    kinetic = mx * u[0] + my * u[1] + mz * u[2]
    return u, (GAMMA - 1.0) * (energy - 0.5 * kinetic), inverse


def flux_along(fields, speed, pressure, direction):
    result = [fields[1 + direction]]
    for k in range(3):
        term = fields[1 + k] * speed
        result.append(term + pressure if k == direction else term)
    result.append((fields[4] + pressure) * speed)
    return result


def rusanov(left, right):
    lu, lp, li = primitive(left)
    ru, rp, ri = primitive(right)
    lf = flux_along(left, lu[2], lp, 2)
    rf = flux_along(right, ru[2], rp, 2)
    signal = jnp.maximum(
        jnp.abs(lu[2]) + jnp.sqrt(GAMMA * lp * li), jnp.abs(ru[2]) + jnp.sqrt(GAMMA * rp * ri)
    )
    return [
        0.5 * (lf[v] + rf[v]) - 0.5 * signal * (right[v] - left[v]) for v in range(5)
    ]


def split(x):
    hi = x.astype(BF16)
    return hi, (x - hi.astype(F32)).astype(BF16)


def dot_nn(a, b):
    return lax.dot_general(a, b, (((1,), (0,)), ((), ())), preferred_element_type=F32)


def dot_nt(a, b):
    return lax.dot_general(a, b, (((1,), (1,)), ((), ())), preferred_element_type=F32)


def dot3(dot, a, b):
    return dot(a[0], b[0]) + dot(a[0], b[1]) + dot(a[1], b[0])


def hot(mask):
    return jnp.where(mask, 1.0, 0.0).astype(BF16)


def iota(shape, dim):
    return lax.broadcasted_iota(jnp.int32, shape, dim)


def volume_first(src, prim, tmp, acc, step):
    t, a = lax.div(step, 8), lax.rem(step, 8)
    at = lambda v, b: pl.ds(pl.multiple_of(v * 512 + a * 64 + b * 8, 8), 8)
    lines = [[] for _ in range(5)]
    for b in range(8):
        fields = [src[t, at(v, b), :] for v in range(5)]
        u, p, _ = primitive(fields)
        prim[at(0, b), :] = u[0]
        prim[at(1, b), :] = u[2]
        prim[at(2, b), :] = p
        for v, value in enumerate(flux_along(fields, u[1], p, 1)):
            lines[v].append(value)
    for v in range(5):
        for b, value in enumerate(derive(lines[v])):
            acc[at(v, b), :] = value
    column = lambda v, c: pl.ds(v * 512 + a * 64 + c, 8, stride=8)
    lines = [[] for _ in range(5)]
    for c in range(8):
        fields = [None] + [src[t, column(v, c), :] for v in range(1, 5)]
        for v, value in enumerate(
            flux_along(fields, prim[column(1, c), :], prim[column(2, c), :], 2)
        ):
            lines[v].append(value)
    for v in range(5):
        for c, value in enumerate(derive(lines[v])):
            tmp[pl.ds(v * 64 + c, 8, stride=8), :] = value
    for v in range(5):
        for b in range(8):
            acc[at(v, b), :] += tmp[v * 64 + b * 8 : v * 64 + b * 8 + 8, :]


def volume_second(src, prim, acc, out, t, b):
    at = lambda v, a: pl.ds(pl.multiple_of(v * 512 + a * 64 + b * 8, 8), 8)
    lines = [[] for _ in range(5)]
    for a in range(8):
        fields = [None] + [src[t, at(v, a), :] for v in range(1, 5)]
        for v, value in enumerate(
            flux_along(fields, prim[at(0, a), :], prim[at(2, a), :], 0)
        ):
            lines[v].append(value)
    for v in range(5):
        for a, value in enumerate(derive(lines[v])):
            out[t, at(v, a), :] = src[t, at(v, a), :] + (acc[at(v, a), :] + value)


def volume(src, out, prim, tmp, acc, tiles):
    for t in tiles:

        def first(a, carry):
            volume_first(src, prim, tmp, acc, t * 8 + a)
            return carry

        def second(b, carry):
            volume_second(src, prim, acc, out, t, b)
            return carry

        lax.fori_loop(0, 8, first, 0)
        lax.fori_loop(0, 8, second, 0)


def face_rows(src, node, dst):
    for t in range(3):
        count = 128 if t < 2 else 64
        rows = [
            src[g, pl.ds(t * 1024 + node, count, stride=8), :]
            for g in range(3)
        ]
        for g in range(3):
            block = rows[g]
            if t == 2:
                block = jnp.concatenate([block, jnp.zeros((64, 128), F32)], axis=0)
            dst[g * 128 : g * 128 + 128, t * 128 : t * 128 + 128] = block.T


def pair(a, b):
    lower = iota(a.shape, 1) < FACE
    return (
        jnp.where(lower, a, pltpu.roll(b, FACE, 1)),
        jnp.where(lower, pltpu.roll(a, FACE, 1), b),
    )


def diagonal(matrix):
    zero = jnp.zeros((FACE, FACE), F32)
    top = jnp.concatenate([matrix, zero], axis=1)
    bottom = jnp.concatenate([zero, matrix], axis=1)
    return jnp.concatenate([top, bottom], axis=0)


def lanes_of(t):
    return (t * 128, 256 + t * 128) if t < 2 else (512, 640)


def put_parts(ref, rows, t, x):
    for start, piece in zip(lanes_of(t), split(x)):
        ref[rows, start : start + 128] = piece


def pick(hots, table):
    y = dot_nn(hots, table[:, 0:256]) + dot_nn(hots, table[:, 256:512])
    z = dot_nn(hots, table[:, 512:768])
    return y, z[:, :128] + z[:, 128:]


def make_table(faces, proj, table, side_ref):
    hi, lo = split(jnp.concatenate([diagonal(proj[0]), diagonal(proj[1])], axis=0))
    both = jnp.concatenate([hi, lo], axis=1)

    def body(g, carry):
        rows = pl.ds(pl.multiple_of(g * 128, 128), 128)
        for t in range(3):
            x, rest = split(faces[rows, t * 128 : t * 128 + 128])
            y = dot_nt(jnp.concatenate([x, x], axis=1), both) + dot_nt(rest, hi)
            sides = (y[:, :128], y[:, 128:])
            for s in range(2):
                at = pl.ds(pl.multiple_of(s * ELEMS + g * 128, 128), 128)
                put_parts(table, at, t, sides[s])
            if side_ref is not None:
                first, second = pair(*sides)
                side_ref[rows, 2 * t * 128 : 2 * t * 128 + 128] = first
                if t < 2:
                    side_ref[rows, 2 * t * 128 + 128 : 2 * t * 128 + 256] = second
        return carry

    lax.fori_loop(0, 3, body, 0)


def message_row(chunk, row):
    return pl.ds(chunk * CHUNK_ROWS + row, ND, stride=MSG)


def gather_chunk(chunk, hots, table, message):
    y, z = pick(hots[...], table)
    lower = iota((ND, 128), 1) < FACE
    for r in range(PAIRS):
        rows = slice(r * ND, r * ND + ND)
        for t in range(2):
            message[message_row(chunk, 2 * r + t), :] = y[rows, t * 128 : t * 128 + 128]
    for pp in range(HALF):
        even = z[2 * pp * ND : 2 * pp * ND + ND, :]
        odd = z[2 * pp * ND + ND : 2 * pp * ND + 2 * ND, :]
        message[message_row(chunk, 12 + pp), :] = jnp.where(lower, even, pltpu.roll(odd, FACE, 1))


def mega(
    owner_ref, row_ref, rproj_ref, sproj_ref, rstate, sstate,
    ru, su,
    rs, ss, prim, tmp, acc,
    faces_s, faces_r, bands, code_out, code_in, codes, seg,
    tab, ltab, lside, rside, hots, seg_hots, sum_hots,
    rout, rin, lout, lin, rflux, rflux_in, arrived, sums,
    load_sem, own_sem, code_sem, trace_sem, send_sem, r_sem, l_sem, back_sem,
):
    mi, mj = lax.axis_index("rotor"), lax.axis_index("stator")
    me = mi * NS + mj
    tiles = lambda ref, t: ref.at[:, pl.ds(t * 128, 128)]
    loads = [
        [
            pltpu.make_async_copy(tiles(state, t), held.at[t], load_sem.at[n, t])
            for t in range(3)
        ]
        for n, (state, held) in enumerate(((rstate, rs), (sstate, ss)))
    ]
    for copy in loads[0] + loads[1]:
        copy.start()

    def coords(d):
        return (lax.div(d, NS), lax.rem(d, NS))

    def peer(p):
        o = lax.rem(p * 37, ND)
        return lax.rem(lax.div(o, NS) + mi, NR), lax.rem(lax.rem(o, NS) + mj, NS)

    barrier = pltpu.get_barrier_semaphore()

    def greet(p, carry):
        pl.semaphore_signal(
            barrier, inc=1, device_id=coords(lax.rem(me + p, ND)), device_id_type=MESH
        )
        return carry

    lax.fori_loop(1, ND, greet, 0)

    owner = owner_ref[...].astype(F32)
    code = row_ref[...]
    lane = iota((1, SEGS), 1)
    side = lax.rem(lane, 2)
    code = code + side * ELEMS + 1
    high = lax.div(code, 4).astype(F32)
    low = lax.rem(code, 4).astype(F32)
    packed = jnp.concatenate([owner, high, low, jnp.zeros((5, SEGS), F32)], axis=0).astype(BF16)
    new = iota((SEGS, SEGS), 0)
    old = iota((SEGS, SEGS), 1)
    order = hot(old == jnp.where(new < ELEMS, 2 * new, 2 * new - 2 * ELEMS + 1))
    by_side = dot_nt(packed, order)
    owner = by_side[0:1]
    member = owner == iota((ND, SEGS), 0).astype(F32)
    member_hot = hot(member)
    earlier = dot_nn(member_hot, hot(new < old))
    rank = jnp.sum(jnp.where(member, earlier, 0.0), axis=0, keepdims=True)
    seg[0:1, :] = owner
    seg[1:2, :] = rank
    seg[2:8, :] = jnp.zeros((6, SEGS), F32)
    ranked = rank == iota((ND, SEGS), 0).astype(F32)
    table = 4.0 * dot_nt(member_hot, jnp.where(ranked, by_side[1:2], 0.0).astype(BF16))
    table = table + dot_nt(member_hot, jnp.where(ranked, by_side[2:3], 0.0).astype(BF16))
    code_out[...] = table.reshape(ND, 1, 128)

    for copy in loads[0]:
        copy.wait()
    face_rows(rs, NODES - 1, faces_r)
    for copy in loads[1]:
        copy.wait()
    face_rows(ss, 0, faces_s)
    make_table(faces_s, sproj_ref, tab, None)

    pl.semaphore_wait(barrier, ND - 1)

    def ring(src, dst, sems, me_rows):
        def send(p, carry):
            i = lax.rem(mi + p, NR)
            pltpu.make_async_remote_copy(
                src_ref=src.at[pl.ds(pl.multiple_of(i * BAND, 16), BAND)],
                dst_ref=dst.at[me_rows],
                send_sem=sems.at[0], recv_sem=sems.at[1],
                device_id=(i, mj), device_id_type=MESH,
            ).start()
            return carry

        lax.fori_loop(1, NR, send, 0)

    def ring_wait(dst, sem):
        rows = dst.at[pl.ds(0, (NR - 1) * BAND)]
        pltpu.make_async_copy(rows, rows, sem).wait()

    my_rows = pl.ds(pl.multiple_of(mi * BAND, 16), BAND)
    ring(faces_r, bands, trace_sem, my_rows)
    def send_code(p, carry):
        i, j = peer(p)
        pltpu.make_async_remote_copy(
            src_ref=code_out.at[i * NS + j], dst_ref=code_in.at[me],
            send_sem=code_sem.at[0], recv_sem=code_sem.at[1],
            device_id=(i, j), device_id_type=MESH,
        ).start()
        return carry

    lax.fori_loop(1, ND, send_code, 0)
    own = pltpu.make_async_copy(code_out.at[me], code_in.at[me], own_sem.at[0])
    own.start()
    own_trace = pltpu.make_async_copy(faces_r.at[my_rows], bands.at[my_rows], own_sem.at[1])
    own_trace.start()

    volume(rs, ru, prim, tmp, acc, range(2))

    own.wait()
    part = code_in.at[pl.ds(0, ND - 1)]
    pltpu.make_async_copy(part, part, code_sem.at[1]).wait()
    codes[...] = code_in[...].reshape(ND, 128)

    def send_chunk(chunk, src, dst, sems):
        def send(p, carry):
            i, j = peer(p)
            at = pl.ds(pl.multiple_of(chunk * CHUNK_ROWS + (i * NS + j) * MSG, MSG), SENT)
            to = pl.ds(pl.multiple_of(chunk * CHUNK_ROWS + me * MSG, MSG), SENT)
            pltpu.make_async_remote_copy(
                src_ref=src.at[at], dst_ref=dst.at[to],
                send_sem=send_sem, recv_sem=sems.at[chunk],
                device_id=(i, j), device_id_type=MESH,
            ).start()
            return carry

        lax.fori_loop(1, ND, send, 0)

    def wait_chunk(chunk, dst, sems):
        rows = dst.at[pl.ds(chunk * CHUNK_ROWS, (ND - 1) * SENT)]
        pltpu.make_async_copy(rows, rows, sems.at[chunk]).wait()

    def own_chunk(chunk, src, dst, sem):
        to = pl.ds(pl.multiple_of(chunk * CHUNK_ROWS + me * MSG, MSG), SENT)
        return pltpu.make_async_copy(src.at[to], dst.at[to], sem)

    for chunk in range(2):
        for r in range(PAIRS):
            slot = chunk * PAIRS + r
            column = codes[:, slot : slot + 1].astype(jnp.int32) - 1
            hots[r * ND : r * ND + ND, :] = hot(column == iota((ND, SEGS), 1))
        gather_chunk(chunk, hots, tab, rout)
        send_chunk(chunk, rout, rin, r_sem)
        own_chunk(chunk, rout, rin, own_sem.at[2 + chunk]).start()

    own_trace.wait()
    ring_wait(bands, trace_sem.at[1])
    make_table(bands, rproj_ref, ltab, lside)
    for chunk in range(2):
        belongs = seg[0:1, :] == iota((ND, SEGS), 0).astype(F32)
        for r in range(PAIRS):
            slot = chunk * PAIRS + r
            hots[r * ND : r * ND + ND, :] = hot(
                jnp.logical_and(belongs, seg[1:2, :] == float(slot))
            )
        gather_chunk(chunk, hots, ltab, lout)
        send_chunk(chunk, lout, lin, l_sem)
        own_chunk(chunk, lout, lin, own_sem.at[4 + chunk]).start()

    columns = seg[...].T.astype(jnp.int32)
    code_rows = codes[...].T.astype(jnp.int32)
    for s in range(2):
        rows = slice(s * ELEMS, s * ELEMS + ELEMS)
        slot = columns[rows, 1:2] * ND + columns[rows, 0:1]
        for r in range(CAP):
            cols = slice(r * ND, r * ND + ND)
            seg_hots[rows, cols] = hot(slot == iota((ELEMS, ND), 1) + r * ND)
            line = code_rows[r : r + 1, :] - (1 + s * ELEMS)
            sum_hots[rows, cols] = hot(line == iota((ELEMS, ND), 0))
    volume(rs, ru, prim, tmp, acc, range(2, 3))
    volume(ss, su, prim, tmp, acc, range(3))

    lower = iota((ND, 128), 1) < FACE
    for chunk in range(2):
        own_chunk(chunk, rout, rin, own_sem.at[2 + chunk]).wait()
        wait_chunk(chunk, rin, r_sem)
        for r in range(PAIRS):
            at = pl.ds((chunk * PAIRS + r) * ND, ND)
            for t in range(2):
                put_parts(arrived, at, t, rin[message_row(chunk, 2 * r + t), :])
            x = rin[message_row(chunk, 12 + r // 2), :]
            if r % 2:
                x = pltpu.roll(x, FACE, 1)
            put_parts(arrived, at, 2, jnp.where(lower, x, 0.0))
    for s in range(2):
        rows = slice(s * ELEMS, s * ELEMS + ELEMS)
        y, z = pick(seg_hots[rows, :], arrived)
        rside[rows, 0:256] = y
        rside[rows, 256:384] = z
    zero = jnp.zeros((FACE, FACE), F32)
    back = []
    for half in range(2):
        blocks = [
            jnp.concatenate([rproj_ref[s], zero] if half == 0 else [zero, rproj_ref[s]], axis=1)
            for s in range(2)
        ]
        back.append(split(jnp.concatenate(blocks, axis=0)))

    def band_flux(g, carry):
        rows = pl.ds(pl.multiple_of(g * 128, 128), 128)
        others = pl.ds(pl.multiple_of(ELEMS + g * 128, 128), 128)
        left = [lside[rows, v * 128 : v * 128 + 128] for v in range(5)]
        right = []
        for t in range(3):
            cols = slice(t * 128, t * 128 + 128)
            right += list(pair(rside[rows, cols], rside[others, cols]))
        flux = [split(x) for x in rusanov(left, right[:5])]
        for t in range(3):
            y = dot3(dot_nn, flux[2 * t], back[0])
            if t < 2:
                y = y + dot3(dot_nn, flux[2 * t + 1], back[1])
            rflux[rows, t * 128 : t * 128 + 128] = y
        return carry

    lax.fori_loop(0, 3, band_flux, 0)
    ring(rflux, rflux_in, back_sem, my_rows)
    own_back = pltpu.make_async_copy(rflux.at[my_rows], rflux_in.at[my_rows], own_sem.at[6])
    own_back.start()

    def fields(ref, chunk, pp):
        tile = lambda r, t: ref[message_row(chunk, 2 * (2 * pp + r) + t), :]
        return [
            *pair(tile(0, 0), tile(1, 0)),
            *pair(tile(0, 1), tile(1, 1)),
            ref[message_row(chunk, 12 + pp), :],
        ]

    for chunk in range(2):
        own_chunk(chunk, lout, lin, own_sem.at[4 + chunk]).wait()
        wait_chunk(chunk, lin, l_sem)
        for pp in range(HALF):
            slot = chunk * PAIRS + 2 * pp
            named = jnp.where(lower, codes[:, slot : slot + 1], codes[:, slot + 1 : slot + 2])
            flux = [
                jnp.where(named > 0.5, x, 0.0)
                for x in rusanov(fields(lin, chunk, pp), fields(rout, chunk, pp))
            ]
            first = [*pair(flux[0], flux[1])], [*pair(flux[2], flux[3])]
            last = (
                jnp.where(lower, flux[4], 0.0),
                jnp.where(lower, pltpu.roll(flux[4], FACE, 1), 0.0),
            )
            for r in range(2):
                at = pl.ds((2 * pp + r) * ND, ND)
                put_parts(arrived, at, 0, first[0][r])
                put_parts(arrived, at, 1, first[1][r])
                put_parts(arrived, at, 2, last[r])
        for s in range(2):
            rows = slice(s * ELEMS, s * ELEMS + ELEMS)
            some = sum_hots[rows, chunk * PAIRS * ND : (chunk + 1) * PAIRS * ND]
            y, z = pick(some, arrived.at[pl.ds(0, PAIRS * ND)])
            if chunk == 0:
                sums[rows, 0:256] = y
                sums[rows, 256:384] = z
            else:
                sums[rows, 0:256] += y
                sums[rows, 256:384] += z

    def face_flux(src, node):
        at = lambda v: pl.ds(v * 512 + node, FACE, stride=8)
        result = [[] for _ in range(5)]
        for g in range(3):
            fields = [src[g, at(v), :] for v in range(5)]
            u, p, _ = primitive(fields)
            for v, value in enumerate(flux_along(fields, u[2], p, 2)):
                result[v].append(value)
        return [jnp.concatenate(r, axis=1) for r in result]

    def add(out, node, v, change):
        for g in range(3):
            at = pl.ds(v * 512 + node, FACE, stride=8)
            out[g, at, :] = out[g, at, :] + change[:, g * 128 : g * 128 + 128]

    adjoint = jnp.concatenate([diagonal(sproj_ref[0]), diagonal(sproj_ref[1])], axis=0)
    adjoint = split(adjoint.T)
    mine = face_flux(ss, 0)
    for t in range(3):
        cols = slice(t * 128, t * 128 + 128)
        both = jnp.concatenate([sums[0:ELEMS, cols], sums[ELEMS : 2 * ELEMS, cols]], axis=1)
        y = dot3(dot_nt, adjoint, split(both))
        for vh in range(2 if t < 2 else 1):
            v = 2 * t + vh
            flux = 0.5 * y[vh * FACE : vh * FACE + FACE, :]
            add(su, 0, v, (TIME_STEP * LIFT) * (flux - mine[v]))

    own_back.wait()
    ring_wait(rflux_in, back_sem.at[1])
    mine = face_flux(rs, NODES - 1)
    for t in range(3):
        turned = jnp.concatenate(
            [rflux_in[g * 128 : g * 128 + 128, t * 128 : t * 128 + 128].T for g in range(3)], axis=1
        )
        for vh in range(2 if t < 2 else 1):
            v = 2 * t + vh
            y = turned[vh * FACE : vh * FACE + FACE, :]
            add(ru, NODES - 1, v, (-TIME_STEP * LIFT) * (0.5 * y - mine[v]))

    part = code_out.at[pl.ds(0, ND - 1)]
    pltpu.make_async_copy(part, part, code_sem.at[0]).wait()
    ring_wait(faces_r, trace_sem.at[0])
    ring_wait(rflux, back_sem.at[0])
    for chunk in range(4):
        rows = rout.at[pl.ds(0, (ND - 1) * SENT)]
        pltpu.make_async_copy(rows, rows, send_sem).wait()


def finish(ru, su, rnext, snext, sem):
    copies = [
        pltpu.make_async_copy(held.at[t], out.at[:, pl.ds(t * 128, 128)], sem.at[n, t])
        for n, (held, out) in enumerate(((ru, rnext), (su, snext)))
        for t in range(3)
    ]
    for copy in copies:
        copy.start()
    for copy in copies:
        copy.wait()


def body(rotor_state, stator_state, rotor_projection, proj_stator, seg_owner, seg_row):
    vmem = pl.BlockSpec(memory_space=pltpu.VMEM)
    hbm = pl.BlockSpec(memory_space=pl.ANY)
    V = pltpu.VMEM
    dma = pltpu.SemaphoreType.DMA
    state = (ROWS, ELEMS)
    held = (3, ROWS, 128)
    big = jax.ShapeDtypeStruct(state, F32)
    parts = pl.pallas_call(
        mega,
        out_shape=(V(held, F32), V(held, F32)),
        in_specs=[vmem, vmem, vmem, vmem, hbm, hbm],
        scratch_shapes=[
            V(held, F32), V(held, F32),
            V((3 * 512, 128), F32), V((320, 128), F32), V((ROWS, 128), F32),
            V((ELEMS, 384), F32), V((ELEMS, 384), F32), V((ELEMS, 384), F32),
            V((ND, 1, 128), F32), V((ND, 1, 128), F32), V((ND, 128), F32), V((8, SEGS), F32),
            V((SEGS, SEGS), BF16), V((SEGS, SEGS), BF16), V((ELEMS, WIDE), F32), V((SEGS, 384), F32),
            V((PAIRS * ND, SEGS), BF16), V((SEGS, CAP * ND), BF16), V((SEGS, CAP * ND), BF16),
            V((2 * CHUNK_ROWS, 128), F32), V((2 * CHUNK_ROWS, 128), F32),
            V((2 * CHUNK_ROWS, 128), F32), V((2 * CHUNK_ROWS, 128), F32),
            V((ELEMS, 384), F32), V((ELEMS, 384), F32),
            V((CAP * ND, SEGS), BF16), V((SEGS, 384), F32),
            dma((2, 3)), dma((7,)), dma((2,)), dma((2,)), dma, dma((2,)), dma((2,)), dma((2,)),
        ],
        compiler_params=pltpu.CompilerParams(
            collective_id=0, has_side_effects=True, vmem_limit_bytes=48 * 2**20
        ),
    )(
        seg_owner.reshape(1, SEGS),
        seg_row.reshape(1, SEGS),
        rotor_projection,
        proj_stator,
        rotor_state.reshape(state),
        stator_state.reshape(state),
    )
    rotor_next, stator_next = pl.pallas_call(
        finish,
        out_shape=(big, big),
        in_specs=[hbm, hbm],
        out_specs=(hbm, hbm),
        scratch_shapes=[dma((2, 3))],
        compiler_params=pltpu.CompilerParams(vmem_limit_bytes=4 * 2**20),
    )(*parts)
    return rotor_next.reshape(rotor_state.shape), stator_next.reshape(stator_state.shape)


def solution(mesh):
    spec = P(None, None, None, None, ("rotor", "stator"))
    in_specs = (spec, spec, P(), P(), P(("rotor", "stator"), None), P(("rotor", "stator")))
    return jax.shard_map(body, mesh=mesh, in_specs=in_specs, out_specs=(spec, spec), check_vma=False)
```

```python
import functools

import jax
import jax.numpy as jnp
import numpy as np
from jax import lax
from jax.experimental import pallas as pl
from jax.experimental.pallas import tpu as pltpu
from jax.sharding import PartitionSpec as P

NODES = 8
FACE = 64
NR = 8
NS = 16
ND = NR * NS
ELEMS = 384
BAND = ELEMS // NR
SEGS = 2 * ELEMS
ROWS = 5 * NODES * FACE
CAP = 12
PAIRS = CAP // 2
HALF = PAIRS // 2
MSG = 16
SENT = 15
CHUNK_ROWS = ND * MSG
WIDE = 5 * 128
GAMMA = 1.4
TIME_STEP = 0.02
LIFT = 28.0
MESH = pl.DeviceIdType.MESH
F32 = jnp.float32
BF16 = jnp.bfloat16


def cheb_matrix():
    degree = NODES - 1
    j = np.arange(degree + 1)
    points = -np.cos(np.pi * j / degree)
    weights = np.where((j == 0) | (j == degree), 2.0, 1.0) * (-1.0) ** j
    spacing = points[:, None] - points[None, :]
    identity = np.eye(degree + 1)
    matrix = weights[:, None] / weights[None, :] / (spacing + identity)
    matrix = matrix - identity * matrix.sum(axis=1)[:, None]
    return matrix.astype(np.float32)


DM = cheb_matrix().astype(np.float64) * (-TIME_STEP * 0.5)
ODD = DM[:4, :4] - DM[:4, :3:-1]
EVEN = DM[:4, :4] + DM[:4, :3:-1]


def derive(line):
    plus = [line[j] + line[7 - j] for j in range(4)]
    minus = [line[j] - line[7 - j] for j in range(4)]
    out = [None] * 8
    for i in range(4):
        p = sum(float(ODD[i, j]) * minus[j] for j in range(4))
        q = sum(float(EVEN[i, j]) * plus[j] for j in range(4))
        out[i] = p + q
        out[7 - i] = p - q
    return out


def primitive(fields):
    density, mx, my, mz, energy = fields
    inverse = 1.0 / density
    u = (mx * inverse, my * inverse, mz * inverse)
    kinetic = mx * u[0] + my * u[1] + mz * u[2]
    return u, (GAMMA - 1.0) * (energy - 0.5 * kinetic), inverse


def flux_along(fields, speed, pressure, direction):
    result = [fields[1 + direction]]
    for k in range(3):
        term = fields[1 + k] * speed
        result.append(term + pressure if k == direction else term)
    result.append((fields[4] + pressure) * speed)
    return result


def rusanov(left, right):
    lu, lp, li = primitive(left)
    ru, rp, ri = primitive(right)
    lf = flux_along(left, lu[2], lp, 2)
    rf = flux_along(right, ru[2], rp, 2)
    signal = jnp.maximum(
        jnp.abs(lu[2]) + jnp.sqrt(GAMMA * lp * li), jnp.abs(ru[2]) + jnp.sqrt(GAMMA * rp * ri)
    )
    return [
        0.5 * (lf[v] + rf[v]) - 0.5 * signal * (right[v] - left[v]) for v in range(5)
    ]


def split(x):
    hi = x.astype(BF16)
    return hi, (x - hi.astype(F32)).astype(BF16)


def dot_nn(a, b):
    return lax.dot_general(a, b, (((1,), (0,)), ((), ())), preferred_element_type=F32)


def dot_nt(a, b):
    return lax.dot_general(a, b, (((1,), (1,)), ((), ())), preferred_element_type=F32)


def dot3(dot, a, b):
    return dot(a[0], b[0]) + dot(a[0], b[1]) + dot(a[1], b[0])


def hot(mask):
    return jnp.where(mask, 1.0, 0.0).astype(BF16)


def iota(shape, dim):
    return lax.broadcasted_iota(jnp.int32, shape, dim)


def volume_first(src, prim, tmp, acc, step):
    t, a = lax.div(step, 8), lax.rem(step, 8)
    at = lambda v, b: pl.ds(pl.multiple_of(v * 512 + a * 64 + b * 8, 8), 8)
    lines = [[] for _ in range(5)]
    for b in range(8):
        fields = [src[t, at(v, b), :] for v in range(5)]
        u, p, _ = primitive(fields)
        prim[at(0, b), :] = u[0]
        prim[at(1, b), :] = u[2]
        prim[at(2, b), :] = p
        for v, value in enumerate(flux_along(fields, u[1], p, 1)):
            lines[v].append(value)
    for v in range(5):
        for b, value in enumerate(derive(lines[v])):
            acc[at(v, b), :] = value
    column = lambda v, c: pl.ds(v * 512 + a * 64 + c, 8, stride=8)
    lines = [[] for _ in range(5)]
    for c in range(8):
        fields = [None] + [src[t, column(v, c), :] for v in range(1, 5)]
        for v, value in enumerate(
            flux_along(fields, prim[column(1, c), :], prim[column(2, c), :], 2)
        ):
            lines[v].append(value)
    for v in range(5):
        for c, value in enumerate(derive(lines[v])):
            tmp[pl.ds(v * 64 + c, 8, stride=8), :] = value
    for v in range(5):
        for b in range(8):
            acc[at(v, b), :] += tmp[v * 64 + b * 8 : v * 64 + b * 8 + 8, :]


def volume_second(src, prim, acc, out, t, b):
    at = lambda v, a: pl.ds(pl.multiple_of(v * 512 + a * 64 + b * 8, 8), 8)
    lines = [[] for _ in range(5)]
    for a in range(8):
        fields = [None] + [src[t, at(v, a), :] for v in range(1, 5)]
        for v, value in enumerate(
            flux_along(fields, prim[at(0, a), :], prim[at(2, a), :], 0)
        ):
            lines[v].append(value)
    for v in range(5):
        for a, value in enumerate(derive(lines[v])):
            out[t, at(v, a), :] = src[t, at(v, a), :] + (acc[at(v, a), :] + value)


def volume(src, out, prim, tmp, acc, tiles):
    for t in tiles:

        def first(a, carry):
            volume_first(src, prim, tmp, acc, t * 8 + a)
            return carry

        def second(b, carry):
            volume_second(src, prim, acc, out, t, b)
            return carry

        lax.fori_loop(0, 8, first, 0)
        lax.fori_loop(0, 8, second, 0)


def face_rows(src, node, dst):
    for t in range(3):
        count = 128 if t < 2 else 64
        rows = [
            src[g, pl.ds(t * 1024 + node, count, stride=8), :]
            for g in range(3)
        ]
        for g in range(3):
            block = rows[g]
            if t == 2:
                block = jnp.concatenate([block, jnp.zeros((64, 128), F32)], axis=0)
            dst[g * 128 : g * 128 + 128, t * 128 : t * 128 + 128] = block.T


def pair(a, b):
    lower = iota(a.shape, 1) < FACE
    return (
        jnp.where(lower, a, pltpu.roll(b, FACE, 1)),
        jnp.where(lower, pltpu.roll(a, FACE, 1), b),
    )


def diagonal(matrix):
    zero = jnp.zeros((FACE, FACE), F32)
    top = jnp.concatenate([matrix, zero], axis=1)
    bottom = jnp.concatenate([zero, matrix], axis=1)
    return jnp.concatenate([top, bottom], axis=0)


def lanes_of(t):
    return (t * 128, 256 + t * 128) if t < 2 else (512, 640)


def put_parts(ref, rows, t, x):
    for start, piece in zip(lanes_of(t), split(x)):
        ref[rows, start : start + 128] = piece


def pick(hots, table):
    y = dot_nn(hots, table[:, 0:256]) + dot_nn(hots, table[:, 256:512])
    z = dot_nn(hots, table[:, 512:768])
    return y, z[:, :128] + z[:, 128:]


def make_table(faces, proj, table, side_ref):
    hi, lo = split(jnp.concatenate([diagonal(proj[0]), diagonal(proj[1])], axis=0))
    both = jnp.concatenate([hi, lo], axis=1)

    def body(g, carry):
        rows = pl.ds(pl.multiple_of(g * 128, 128), 128)
        for t in range(3):
            x, rest = split(faces[rows, t * 128 : t * 128 + 128])
            y = dot_nt(jnp.concatenate([x, x], axis=1), both) + dot_nt(rest, hi)
            sides = (y[:, :128], y[:, 128:])
            for s in range(2):
                at = pl.ds(pl.multiple_of(s * ELEMS + g * 128, 128), 128)
                put_parts(table, at, t, sides[s])
            if side_ref is not None:
                first, second = pair(*sides)
                side_ref[rows, 2 * t * 128 : 2 * t * 128 + 128] = first
                if t < 2:
                    side_ref[rows, 2 * t * 128 + 128 : 2 * t * 128 + 256] = second
        return carry

    lax.fori_loop(0, 3, body, 0)


def pack_last(faces, packed):
    lower = iota((BAND // 2, 128), 1) < FACE
    for i in range(NR):
        first = faces[i * BAND : i * BAND + BAND // 2, 256:384]
        second = faces[i * BAND + BAND // 2 : i * BAND + BAND, 256:384]
        packed[i * BAND // 2 : (i + 1) * BAND // 2, :] = jnp.where(
            lower, first, pltpu.roll(second, FACE, 1)
        )


def unpack_last(packed, faces):
    lower = iota((BAND // 2, 128), 1) < FACE
    for i in range(NR):
        x = packed[i * BAND // 2 : (i + 1) * BAND // 2, :]
        faces[i * BAND : i * BAND + BAND // 2, 256:384] = jnp.where(lower, x, 0.0)
        faces[i * BAND + BAND // 2 : i * BAND + BAND, 256:384] = jnp.where(
            lower, pltpu.roll(x, FACE, 1), 0.0
        )


def message_row(chunk, row):
    return pl.ds(chunk * CHUNK_ROWS + row, ND, stride=MSG)


def gather_chunk(chunk, hots, table, message):
    y, z = pick(hots[...], table)
    lower = iota((ND, 128), 1) < FACE
    for r in range(PAIRS):
        rows = slice(r * ND, r * ND + ND)
        for t in range(2):
            message[message_row(chunk, 2 * r + t), :] = y[rows, t * 128 : t * 128 + 128]
    for pp in range(HALF):
        even = z[2 * pp * ND : 2 * pp * ND + ND, :]
        odd = z[2 * pp * ND + ND : 2 * pp * ND + 2 * ND, :]
        message[message_row(chunk, 12 + pp), :] = jnp.where(lower, even, pltpu.roll(odd, FACE, 1))


def mega(
    owner_ref, row_ref, rproj_ref, sproj_ref, rstate, sstate,
    ru, su,
    rs, ss, prim, tmp, acc,
    faces_s, faces_r, bands, code_out, code_in, codes, seg,
    tab, ltab, lside, rside, hots, seg_hots, sum_hots,
    rout, rin, lout, lin, rflux, rflux_in, last_out, last_in, last_back, arrived, sums,
    load_sem, own_sem, code_sem, trace_sem, send_sem, r_sem, l_sem, back_sem,
):
    mi, mj = lax.axis_index("rotor"), lax.axis_index("stator")
    me = mi * NS + mj
    tiles = lambda ref, t: ref.at[:, pl.ds(t * 128, 128)]
    loads = [
        [
            pltpu.make_async_copy(tiles(state, t), held.at[t], load_sem.at[n, t])
            for t in range(3)
        ]
        for n, (state, held) in enumerate(((rstate, rs), (sstate, ss)))
    ]
    for copy in loads[0] + loads[1]:
        copy.start()

    def coords(d):
        return (lax.div(d, NS), lax.rem(d, NS))

    def peer(p):
        o = lax.rem(p * 37, ND)
        return lax.rem(lax.div(o, NS) + mi, NR), lax.rem(lax.rem(o, NS) + mj, NS)

    barrier = pltpu.get_barrier_semaphore()

    def greet(p, carry):
        pl.semaphore_signal(
            barrier, inc=1, device_id=coords(lax.rem(me + p, ND)), device_id_type=MESH
        )
        return carry

    lax.fori_loop(1, ND, greet, 0)

    owner = owner_ref[...].astype(F32)
    code = row_ref[...].reshape(1, SEGS)
    lane = iota((1, SEGS), 1)
    side = lax.rem(lane, 2)
    code = code + side * ELEMS + 1
    high = lax.div(code, 4).astype(F32)
    low = lax.rem(code, 4).astype(F32)
    packed = jnp.concatenate([owner, high, low, jnp.zeros((5, SEGS), F32)], axis=0).astype(BF16)
    new = iota((SEGS, SEGS), 0)
    old = iota((SEGS, SEGS), 1)
    order = hot(old == jnp.where(new < ELEMS, 2 * new, 2 * new - 2 * ELEMS + 1))
    by_side = dot_nt(packed, order)
    owner = by_side[0:1]
    member = owner == iota((ND, SEGS), 0).astype(F32)
    member_hot = hot(member)
    earlier = dot_nn(member_hot, hot(new < old))
    rank = jnp.sum(jnp.where(member, earlier, 0.0), axis=0, keepdims=True)
    seg[0:1, :] = owner
    seg[1:2, :] = rank
    seg[2:8, :] = jnp.zeros((6, SEGS), F32)
    ranked = rank == iota((ND, SEGS), 0).astype(F32)
    table = 4.0 * dot_nt(member_hot, jnp.where(ranked, by_side[1:2], 0.0).astype(BF16))
    table = table + dot_nt(member_hot, jnp.where(ranked, by_side[2:3], 0.0).astype(BF16))
    code_out[...] = table.reshape(ND, 1, 128)

    for copy in loads[0]:
        copy.wait()
    face_rows(rs, NODES - 1, faces_r)
    pack_last(faces_r, last_out)
    for copy in loads[1]:
        copy.wait()
    face_rows(ss, 0, faces_s)
    make_table(faces_s, sproj_ref, tab, None)

    pl.semaphore_wait(barrier, ND - 1)

    block = lambda ref, i: ref.at[pl.ds(pl.multiple_of(i * BAND, 16), BAND), pl.ds(0, 256)]
    tail_block = lambda ref, i: ref.at[pl.ds(pl.multiple_of(i * BAND // 2, 8), BAND // 2)]

    def ring_send(i, src, dst, src_last, dst_last, sems):
        for n, (cut, a, b) in enumerate(((block, src, dst), (tail_block, src_last, dst_last))):
            pltpu.make_async_remote_copy(
                src_ref=cut(a, i), dst_ref=cut(b, mi),
                send_sem=sems.at[0, n], recv_sem=sems.at[1, n],
                device_id=(i, mj), device_id_type=MESH,
            ).start()

    def ring_wait(dst, dst_last, sems, side):
        rows = dst.at[pl.ds(0, (NR - 1) * BAND), pl.ds(0, 256)]
        pltpu.make_async_copy(rows, rows, sems.at[side, 0]).wait()
        rows = dst_last.at[pl.ds(0, (NR - 1) * BAND // 2)]
        pltpu.make_async_copy(rows, rows, sems.at[side, 1]).wait()

    def ring_own(src, dst, src_last, dst_last, n):
        return [
            pltpu.make_async_copy(block(src, mi), block(dst, mi), own_sem.at[n]),
            pltpu.make_async_copy(tail_block(src_last, mi), tail_block(dst_last, mi), own_sem.at[n + 1]),
        ]

    def send_code(p, carry):
        i, j = peer(p)
        pltpu.make_async_remote_copy(
            src_ref=code_out.at[i * NS + j], dst_ref=code_in.at[me],
            send_sem=code_sem.at[0], recv_sem=code_sem.at[1],
            device_id=(i, j), device_id_type=MESH,
        ).start()
        return carry

    def send_trace(p, carry):
        ring_send(lax.rem(mi + p, NR), faces_r, bands, last_out, last_in, trace_sem)
        return carry

    lax.fori_loop(1, ND, send_code, 0)
    lax.fori_loop(1, NR, send_trace, 0)
    own = pltpu.make_async_copy(code_out.at[me], code_in.at[me], own_sem.at[0])
    own.start()
    own_trace = ring_own(faces_r, bands, last_out, last_in, 6)
    for copy in own_trace:
        copy.start()

    volume(rs, ru, prim, tmp, acc, range(2))

    own.wait()
    part = code_in.at[pl.ds(0, ND - 1)]
    pltpu.make_async_copy(part, part, code_sem.at[1]).wait()
    codes[...] = code_in[...].reshape(ND, 128)

    def send_chunk(chunk, src, dst, sems):
        def send(p, carry):
            i, j = peer(p)
            at = pl.ds(pl.multiple_of(chunk * CHUNK_ROWS + (i * NS + j) * MSG, MSG), SENT)
            to = pl.ds(pl.multiple_of(chunk * CHUNK_ROWS + me * MSG, MSG), SENT)
            pltpu.make_async_remote_copy(
                src_ref=src.at[at], dst_ref=dst.at[to],
                send_sem=send_sem, recv_sem=sems.at[chunk],
                device_id=(i, j), device_id_type=MESH,
            ).start()
            return carry

        lax.fori_loop(1, ND, send, 0)

    def wait_chunk(chunk, dst, sems):
        rows = dst.at[pl.ds(chunk * CHUNK_ROWS, (ND - 1) * SENT)]
        pltpu.make_async_copy(rows, rows, sems.at[chunk]).wait()

    def own_chunk(chunk, src, dst, sem):
        to = pl.ds(pl.multiple_of(chunk * CHUNK_ROWS + me * MSG, MSG), SENT)
        return pltpu.make_async_copy(src.at[to], dst.at[to], sem)

    for chunk in range(2):
        for r in range(PAIRS):
            slot = chunk * PAIRS + r
            column = codes[:, slot : slot + 1].astype(jnp.int32) - 1
            hots[r * ND : r * ND + ND, :] = hot(column == iota((ND, SEGS), 1))
        gather_chunk(chunk, hots, tab, rout)
        send_chunk(chunk, rout, rin, r_sem)
        own_chunk(chunk, rout, rin, own_sem.at[2 + chunk]).start()

    for copy in own_trace:
        copy.wait()
    ring_wait(bands, last_in, trace_sem, 1)
    unpack_last(last_in, bands)
    make_table(bands, rproj_ref, ltab, lside)
    for chunk in range(2):
        belongs = seg[0:1, :] == iota((ND, SEGS), 0).astype(F32)
        for r in range(PAIRS):
            slot = chunk * PAIRS + r
            hots[r * ND : r * ND + ND, :] = hot(
                jnp.logical_and(belongs, seg[1:2, :] == float(slot))
            )
        gather_chunk(chunk, hots, ltab, lout)
        send_chunk(chunk, lout, lin, l_sem)
        own_chunk(chunk, lout, lin, own_sem.at[4 + chunk]).start()

    columns = seg[...].T.astype(jnp.int32)
    code_rows = codes[...].T.astype(jnp.int32)
    for s in range(2):
        rows = slice(s * ELEMS, s * ELEMS + ELEMS)
        slot = columns[rows, 1:2] * ND + columns[rows, 0:1]
        for r in range(CAP):
            cols = slice(r * ND, r * ND + ND)
            seg_hots[rows, cols] = hot(slot == iota((ELEMS, ND), 1) + r * ND)
            line = code_rows[r : r + 1, :] - (1 + s * ELEMS)
            sum_hots[rows, cols] = hot(line == iota((ELEMS, ND), 0))
    volume(rs, ru, prim, tmp, acc, range(2, 3))
    volume(ss, su, prim, tmp, acc, range(3))

    lower = iota((ND, 128), 1) < FACE
    for chunk in range(2):
        own_chunk(chunk, rout, rin, own_sem.at[2 + chunk]).wait()
        wait_chunk(chunk, rin, r_sem)
        for r in range(PAIRS):
            at = pl.ds((chunk * PAIRS + r) * ND, ND)
            for t in range(2):
                put_parts(arrived, at, t, rin[message_row(chunk, 2 * r + t), :])
            x = rin[message_row(chunk, 12 + r // 2), :]
            if r % 2:
                x = pltpu.roll(x, FACE, 1)
            put_parts(arrived, at, 2, jnp.where(lower, x, 0.0))
    for s in range(2):
        rows = slice(s * ELEMS, s * ELEMS + ELEMS)
        y, z = pick(seg_hots[rows, :], arrived)
        rside[rows, 0:256] = y
        rside[rows, 256:384] = z
    zero = jnp.zeros((FACE, FACE), F32)
    back = []
    for half in range(2):
        blocks = [
            jnp.concatenate([rproj_ref[s], zero] if half == 0 else [zero, rproj_ref[s]], axis=1)
            for s in range(2)
        ]
        back.append(split(jnp.concatenate(blocks, axis=0)))

    def band_flux(g, carry):
        rows = pl.ds(pl.multiple_of(g * 128, 128), 128)
        others = pl.ds(pl.multiple_of(ELEMS + g * 128, 128), 128)
        left = [lside[rows, v * 128 : v * 128 + 128] for v in range(5)]
        right = []
        for t in range(3):
            cols = slice(t * 128, t * 128 + 128)
            right += list(pair(rside[rows, cols], rside[others, cols]))
        flux = [split(x) for x in rusanov(left, right[:5])]
        for t in range(3):
            y = dot3(dot_nn, flux[2 * t], back[0])
            if t < 2:
                y = y + dot3(dot_nn, flux[2 * t + 1], back[1])
            rflux[rows, t * 128 : t * 128 + 128] = y
        return carry

    lax.fori_loop(0, 3, band_flux, 0)
    ring_wait(faces_r, last_out, trace_sem, 0)
    pack_last(rflux, last_out)

    def send_back(p, carry):
        ring_send(lax.rem(mi + p, NR), rflux, rflux_in, last_out, last_back, back_sem)
        return carry

    lax.fori_loop(1, NR, send_back, 0)
    own_back = ring_own(rflux, rflux_in, last_out, last_back, 8)
    for copy in own_back:
        copy.start()

    def fields(ref, chunk, pp):
        tile = lambda r, t: ref[message_row(chunk, 2 * (2 * pp + r) + t), :]
        return [
            *pair(tile(0, 0), tile(1, 0)),
            *pair(tile(0, 1), tile(1, 1)),
            ref[message_row(chunk, 12 + pp), :],
        ]

    for chunk in range(2):
        own_chunk(chunk, lout, lin, own_sem.at[4 + chunk]).wait()
        wait_chunk(chunk, lin, l_sem)
        for pp in range(HALF):
            slot = chunk * PAIRS + 2 * pp
            named = jnp.where(lower, codes[:, slot : slot + 1], codes[:, slot + 1 : slot + 2])
            flux = [
                jnp.where(named > 0.5, x, 0.0)
                for x in rusanov(fields(lin, chunk, pp), fields(rout, chunk, pp))
            ]
            first = [*pair(flux[0], flux[1])], [*pair(flux[2], flux[3])]
            last = (
                jnp.where(lower, flux[4], 0.0),
                jnp.where(lower, pltpu.roll(flux[4], FACE, 1), 0.0),
            )
            for r in range(2):
                at = pl.ds((2 * pp + r) * ND, ND)
                put_parts(arrived, at, 0, first[0][r])
                put_parts(arrived, at, 1, first[1][r])
                put_parts(arrived, at, 2, last[r])
        for s in range(2):
            rows = slice(s * ELEMS, s * ELEMS + ELEMS)
            some = sum_hots[rows, chunk * PAIRS * ND : (chunk + 1) * PAIRS * ND]
            y, z = pick(some, arrived.at[pl.ds(0, PAIRS * ND)])
            if chunk == 0:
                sums[rows, 0:256] = y
                sums[rows, 256:384] = z
            else:
                sums[rows, 0:256] += y
                sums[rows, 256:384] += z

    def face_flux(src, node):
        at = lambda v: pl.ds(v * 512 + node, FACE, stride=8)
        result = [[] for _ in range(5)]
        for g in range(3):
            fields = [src[g, at(v), :] for v in range(5)]
            u, p, _ = primitive(fields)
            for v, value in enumerate(flux_along(fields, u[2], p, 2)):
                result[v].append(value)
        return [jnp.concatenate(r, axis=1) for r in result]

    def add(out, node, v, change):
        for g in range(3):
            at = pl.ds(v * 512 + node, FACE, stride=8)
            out[g, at, :] = out[g, at, :] + change[:, g * 128 : g * 128 + 128]

    adjoint = jnp.concatenate([diagonal(sproj_ref[0]), diagonal(sproj_ref[1])], axis=0)
    adjoint = split(adjoint.T)
    mine = face_flux(ss, 0)
    for t in range(3):
        cols = slice(t * 128, t * 128 + 128)
        both = jnp.concatenate([sums[0:ELEMS, cols], sums[ELEMS : 2 * ELEMS, cols]], axis=1)
        y = dot3(dot_nt, adjoint, split(both))
        for vh in range(2 if t < 2 else 1):
            v = 2 * t + vh
            flux = 0.5 * y[vh * FACE : vh * FACE + FACE, :]
            add(su, 0, v, (TIME_STEP * LIFT) * (flux - mine[v]))

    for copy in own_back:
        copy.wait()
    ring_wait(rflux_in, last_back, back_sem, 1)
    unpack_last(last_back, rflux_in)
    mine = face_flux(rs, NODES - 1)
    for t in range(3):
        turned = jnp.concatenate(
            [rflux_in[g * 128 : g * 128 + 128, t * 128 : t * 128 + 128].T for g in range(3)], axis=1
        )
        for vh in range(2 if t < 2 else 1):
            v = 2 * t + vh
            y = turned[vh * FACE : vh * FACE + FACE, :]
            add(ru, NODES - 1, v, (-TIME_STEP * LIFT) * (0.5 * y - mine[v]))

    part = code_out.at[pl.ds(0, ND - 1)]
    pltpu.make_async_copy(part, part, code_sem.at[0]).wait()
    ring_wait(rflux, last_out, back_sem, 0)
    for chunk in range(4):
        rows = rout.at[pl.ds(0, (ND - 1) * SENT)]
        pltpu.make_async_copy(rows, rows, send_sem).wait()


def finish(ru, su, rnext, snext, sem):
    copies = [
        pltpu.make_async_copy(
            held.at[t, pl.ds(v * 512, 512)],
            out.at[pl.ds(v * 512, 512), pl.ds(t * 128, 128)],
            sem.at[n, t, v],
        )
        for n, (held, out) in enumerate(((ru, rnext), (su, snext)))
        for v in range(5)
        for t in range(3)
    ]
    for copy in copies:
        copy.start()
    for copy in copies:
        copy.wait()


def body(rotor_state, stator_state, rotor_projection, proj_stator, seg_owner, seg_row):
    vmem = pl.BlockSpec(memory_space=pltpu.VMEM)
    hbm = pl.BlockSpec(memory_space=pl.ANY)
    V = pltpu.VMEM
    dma = pltpu.SemaphoreType.DMA
    state = (ROWS, ELEMS)
    held = (3, ROWS, 128)
    big = jax.ShapeDtypeStruct(state, F32)
    parts = pl.pallas_call(
        mega,
        out_shape=(V(held, F32), V(held, F32)),
        in_specs=[vmem, vmem, vmem, vmem, hbm, hbm],
        scratch_shapes=[
            V(held, F32), V(held, F32),
            V((3 * 512, 128), F32), V((320, 128), F32), V((ROWS, 128), F32),
            V((ELEMS, 384), F32), V((ELEMS, 384), F32), V((ELEMS, 384), F32),
            V((ND, 1, 128), F32), V((ND, 1, 128), F32), V((ND, 128), F32), V((8, SEGS), F32),
            V((SEGS, SEGS), BF16), V((SEGS, SEGS), BF16), V((ELEMS, WIDE), F32), V((SEGS, 384), F32),
            V((PAIRS * ND, SEGS), BF16), V((SEGS, CAP * ND), BF16), V((SEGS, CAP * ND), BF16),
            V((2 * CHUNK_ROWS, 128), F32), V((2 * CHUNK_ROWS, 128), F32),
            V((2 * CHUNK_ROWS, 128), F32), V((2 * CHUNK_ROWS, 128), F32),
            V((ELEMS, 384), F32), V((ELEMS, 384), F32),
            V((ELEMS // 2, 128), F32), V((ELEMS // 2, 128), F32), V((ELEMS // 2, 128), F32),
            V((CAP * ND, SEGS), BF16), V((SEGS, 384), F32),
            dma((2, 3)), dma((10,)), dma((2,)), dma((2, 2)), dma, dma((2,)), dma((2,)), dma((2, 2)),
        ],
        compiler_params=pltpu.CompilerParams(
            collective_id=0, has_side_effects=True, vmem_limit_bytes=48 * 2**20
        ),
    )(
        seg_owner.reshape(1, SEGS),
        seg_row,
        rotor_projection,
        proj_stator,
        rotor_state.reshape(state),
        stator_state.reshape(state),
    )
    rotor_next, stator_next = pl.pallas_call(
        finish,
        out_shape=(big, big),
        in_specs=[hbm, hbm],
        out_specs=(hbm, hbm),
        scratch_shapes=[dma((2, 3, 5))],
        compiler_params=pltpu.CompilerParams(vmem_limit_bytes=4 * 2**20),
    )(*parts)
    return rotor_next.reshape(rotor_state.shape), stator_next.reshape(stator_state.shape)


def solution(mesh):
    spec = P(None, None, None, None, ("rotor", "stator"))
    in_specs = (spec, spec, P(), P(), P(("rotor", "stator"), None), P(("rotor", "stator")))
    return jax.shard_map(body, mesh=mesh, in_specs=in_specs, out_specs=(spec, spec), check_vma=False)
```

```python
import functools

import jax
import jax.numpy as jnp
import numpy as np
from jax import lax
from jax.experimental import pallas as pl
from jax.experimental.pallas import tpu as pltpu
from jax.sharding import PartitionSpec as P

NODES = 8
FACE = 64
NR = 8
NS = 16
ND = NR * NS
ELEMS = 384
BAND = ELEMS // NR
SEGS = 2 * ELEMS
ROWS = 5 * NODES * FACE
CAP = 12
PAIRS = CAP // 2
HALF = PAIRS // 2
MSG = 16
SENT = 15
CHUNK_ROWS = ND * MSG
WIDE = 5 * 128
GAMMA = 1.4
TIME_STEP = 0.02
LIFT = 28.0
MESH = pl.DeviceIdType.MESH
F32 = jnp.float32
BF16 = jnp.bfloat16


def cheb_matrix():
    degree = NODES - 1
    j = np.arange(degree + 1)
    points = -np.cos(np.pi * j / degree)
    weights = np.where((j == 0) | (j == degree), 2.0, 1.0) * (-1.0) ** j
    spacing = points[:, None] - points[None, :]
    identity = np.eye(degree + 1)
    matrix = weights[:, None] / weights[None, :] / (spacing + identity)
    matrix = matrix - identity * matrix.sum(axis=1)[:, None]
    return matrix.astype(np.float32)


DM = cheb_matrix().astype(np.float64) * (-TIME_STEP * 0.5)
ODD = DM[:4, :4] - DM[:4, :3:-1]
EVEN = DM[:4, :4] + DM[:4, :3:-1]


def derive(line):
    plus = [line[j] + line[7 - j] for j in range(4)]
    minus = [line[j] - line[7 - j] for j in range(4)]
    out = [None] * 8
    for i in range(4):
        p = sum(float(ODD[i, j]) * minus[j] for j in range(4))
        q = sum(float(EVEN[i, j]) * plus[j] for j in range(4))
        out[i] = p + q
        out[7 - i] = p - q
    return out


def primitive(fields):
    density, mx, my, mz, energy = fields
    inverse = 1.0 / density
    u = (mx * inverse, my * inverse, mz * inverse)
    kinetic = mx * u[0] + my * u[1] + mz * u[2]
    return u, (GAMMA - 1.0) * (energy - 0.5 * kinetic), inverse


def flux_along(fields, speed, pressure, direction):
    result = [fields[1 + direction]]
    for k in range(3):
        term = fields[1 + k] * speed
        result.append(term + pressure if k == direction else term)
    result.append((fields[4] + pressure) * speed)
    return result


def rusanov(left, right):
    lu, lp, li = primitive(left)
    ru, rp, ri = primitive(right)
    lf = flux_along(left, lu[2], lp, 2)
    rf = flux_along(right, ru[2], rp, 2)
    signal = jnp.maximum(
        jnp.abs(lu[2]) + jnp.sqrt(GAMMA * lp * li), jnp.abs(ru[2]) + jnp.sqrt(GAMMA * rp * ri)
    )
    return [
        0.5 * (lf[v] + rf[v]) - 0.5 * signal * (right[v] - left[v]) for v in range(5)
    ]


def split(x):
    hi = x.astype(BF16)
    return hi, (x - hi.astype(F32)).astype(BF16)


def dot_nn(a, b):
    return lax.dot_general(a, b, (((1,), (0,)), ((), ())), preferred_element_type=F32)


def dot_nt(a, b):
    return lax.dot_general(a, b, (((1,), (1,)), ((), ())), preferred_element_type=F32)


def dot3(dot, a, b):
    return dot(a[0], b[0]) + dot(a[0], b[1]) + dot(a[1], b[0])


def hot(mask):
    return jnp.where(mask, 1.0, 0.0).astype(BF16)


def iota(shape, dim):
    return lax.broadcasted_iota(jnp.int32, shape, dim)


def volume_first(src, prim, tmp, acc, step):
    t, a = lax.div(step, 8), lax.rem(step, 8)
    at = lambda v, b: pl.ds(pl.multiple_of(v * 512 + a * 64 + b * 8, 8), 8)
    lines = [[] for _ in range(5)]
    for b in range(8):
        fields = [src[t, at(v, b), :] for v in range(5)]
        u, p, _ = primitive(fields)
        prim[at(0, b), :] = u[0]
        prim[at(1, b), :] = u[2]
        prim[at(2, b), :] = p
        for v, value in enumerate(flux_along(fields, u[1], p, 1)):
            lines[v].append(value)
    for v in range(5):
        for b, value in enumerate(derive(lines[v])):
            acc[at(v, b), :] = value
    column = lambda v, c: pl.ds(v * 512 + a * 64 + c, 8, stride=8)
    lines = [[] for _ in range(5)]
    for c in range(8):
        fields = [None] + [src[t, column(v, c), :] for v in range(1, 5)]
        for v, value in enumerate(
            flux_along(fields, prim[column(1, c), :], prim[column(2, c), :], 2)
        ):
            lines[v].append(value)
    for v in range(5):
        for c, value in enumerate(derive(lines[v])):
            tmp[pl.ds(v * 64 + c, 8, stride=8), :] = value
    for v in range(5):
        for b in range(8):
            acc[at(v, b), :] += tmp[v * 64 + b * 8 : v * 64 + b * 8 + 8, :]


def volume_second(src, prim, acc, out, t, b):
    at = lambda v, a: pl.ds(pl.multiple_of(v * 512 + a * 64 + b * 8, 8), 8)
    lines = [[] for _ in range(5)]
    for a in range(8):
        fields = [None] + [src[t, at(v, a), :] for v in range(1, 5)]
        for v, value in enumerate(
            flux_along(fields, prim[at(0, a), :], prim[at(2, a), :], 0)
        ):
            lines[v].append(value)
    for v in range(5):
        for a, value in enumerate(derive(lines[v])):
            out[t, at(v, a), :] = src[t, at(v, a), :] + (acc[at(v, a), :] + value)


def volume(src, out, prim, tmp, acc, tiles):
    for t in tiles:

        def first(a, carry):
            volume_first(src, prim, tmp, acc, t * 8 + a)
            return carry

        def second(b, carry):
            volume_second(src, prim, acc, out, t, b)
            return carry

        lax.fori_loop(0, 8, first, 0)
        lax.fori_loop(0, 8, second, 0)


def face_rows(src, node, dst):
    for t in range(3):
        count = 128 if t < 2 else 64
        rows = [
            src[g, pl.ds(t * 1024 + node, count, stride=8), :]
            for g in range(3)
        ]
        for g in range(3):
            block = rows[g]
            if t == 2:
                block = jnp.concatenate([block, jnp.zeros((64, 128), F32)], axis=0)
            dst[g * 128 : g * 128 + 128, t * 128 : t * 128 + 128] = block.T


def pair(a, b):
    lower = iota(a.shape, 1) < FACE
    return (
        jnp.where(lower, a, pltpu.roll(b, FACE, 1)),
        jnp.where(lower, pltpu.roll(a, FACE, 1), b),
    )


def diagonal(matrix):
    zero = jnp.zeros((FACE, FACE), F32)
    top = jnp.concatenate([matrix, zero], axis=1)
    bottom = jnp.concatenate([zero, matrix], axis=1)
    return jnp.concatenate([top, bottom], axis=0)


def lanes_of(t):
    return (t * 128, 256 + t * 128) if t < 2 else (512, 640)


def put_parts(ref, rows, t, x):
    for start, piece in zip(lanes_of(t), split(x)):
        ref[rows, start : start + 128] = piece


def pick(hots, table):
    y = dot_nn(hots, table[:, 0:256]) + dot_nn(hots, table[:, 256:512])
    z = dot_nn(hots, table[:, 512:768])
    return y, z[:, :128] + z[:, 128:]


def make_table(faces, proj, table, side_ref):
    hi, lo = split(jnp.concatenate([diagonal(proj[0]), diagonal(proj[1])], axis=0))
    both = jnp.concatenate([hi, lo], axis=1)

    def body(g, carry):
        rows = pl.ds(pl.multiple_of(g * 128, 128), 128)
        for t in range(3):
            x, rest = split(faces[rows, t * 128 : t * 128 + 128])
            y = dot_nt(jnp.concatenate([x, x], axis=1), both) + dot_nt(rest, hi)
            sides = (y[:, :128], y[:, 128:])
            for s in range(2):
                at = pl.ds(pl.multiple_of(s * ELEMS + g * 128, 128), 128)
                put_parts(table, at, t, sides[s])
            if side_ref is not None:
                first, second = pair(*sides)
                side_ref[rows, 2 * t * 128 : 2 * t * 128 + 128] = first
                if t < 2:
                    side_ref[rows, 2 * t * 128 + 128 : 2 * t * 128 + 256] = second
        return carry

    lax.fori_loop(0, 3, body, 0)


def pack_last(faces, packed):
    lower = iota((BAND // 2, 128), 1) < FACE
    for i in range(NR):
        first = faces[i * BAND : i * BAND + BAND // 2, 256:384]
        second = faces[i * BAND + BAND // 2 : i * BAND + BAND, 256:384]
        packed[i * BAND // 2 : (i + 1) * BAND // 2, :] = jnp.where(
            lower, first, pltpu.roll(second, FACE, 1)
        )


def unpack_last(packed, faces):
    lower = iota((BAND // 2, 128), 1) < FACE
    for i in range(NR):
        x = packed[i * BAND // 2 : (i + 1) * BAND // 2, :]
        faces[i * BAND : i * BAND + BAND // 2, 256:384] = jnp.where(lower, x, 0.0)
        faces[i * BAND + BAND // 2 : i * BAND + BAND, 256:384] = jnp.where(
            lower, pltpu.roll(x, FACE, 1), 0.0
        )


def message_row(chunk, row):
    return pl.ds(chunk * CHUNK_ROWS + row, ND, stride=MSG)


def gather_chunk(chunk, hots, table, message):
    y, z = pick(hots[...], table)
    lower = iota((ND, 128), 1) < FACE
    for r in range(PAIRS):
        rows = slice(r * ND, r * ND + ND)
        for t in range(2):
            message[message_row(chunk, 2 * r + t), :] = y[rows, t * 128 : t * 128 + 128]
    for pp in range(HALF):
        even = z[2 * pp * ND : 2 * pp * ND + ND, :]
        odd = z[2 * pp * ND + ND : 2 * pp * ND + 2 * ND, :]
        message[message_row(chunk, 12 + pp), :] = jnp.where(lower, even, pltpu.roll(odd, FACE, 1))


def mega(
    owner_ref, row_ref, rproj_ref, sproj_ref, rstate, sstate,
    ru, su,
    rs, ss, prim, tmp, acc,
    faces_s, faces_r, bands, code_out, code_in, codes, seg,
    tab, ltab, lside, rside, hots, seg_hots, sum_hots,
    rout, rin, lout, lin, rflux, rflux_in, last_out, last_in, last_back, arrived, sums,
    load_sem, own_sem, code_sem, trace_sem, send_sem, r_sem, l_sem, back_sem,
):
    mi, mj = lax.axis_index("rotor"), lax.axis_index("stator")
    me = mi * NS + mj
    tiles = lambda ref, t: ref.at[:, pl.ds(t * 128, 128)]
    loads = [
        [
            pltpu.make_async_copy(tiles(state, t), held.at[t], load_sem.at[n, t])
            for t in range(3)
        ]
        for n, (state, held) in enumerate(((rstate, rs), (sstate, ss)))
    ]
    for copy in loads[0] + loads[1]:
        copy.start()

    def coords(d):
        return (lax.div(d, NS), lax.rem(d, NS))

    def peer(p):
        o = lax.rem(p * 53, ND)
        return lax.rem(lax.div(o, NS) + mi, NR), lax.rem(lax.rem(o, NS) + mj, NS)

    barrier = pltpu.get_barrier_semaphore()

    def greet(p, carry):
        pl.semaphore_signal(
            barrier, inc=1, device_id=coords(lax.rem(me + p, ND)), device_id_type=MESH
        )
        return carry

    lax.fori_loop(1, ND, greet, 0)

    owner = owner_ref[...].astype(F32)
    code = row_ref[...].reshape(1, SEGS)
    lane = iota((1, SEGS), 1)
    side = lax.rem(lane, 2)
    code = code + side * ELEMS + 1
    high = lax.div(code, 4).astype(F32)
    low = lax.rem(code, 4).astype(F32)
    packed = jnp.concatenate([owner, high, low, jnp.zeros((5, SEGS), F32)], axis=0).astype(BF16)
    new = iota((SEGS, SEGS), 0)
    old = iota((SEGS, SEGS), 1)
    order = hot(old == jnp.where(new < ELEMS, 2 * new, 2 * new - 2 * ELEMS + 1))
    by_side = dot_nt(packed, order)
    owner = by_side[0:1]
    member = owner == iota((ND, SEGS), 0).astype(F32)
    member_hot = hot(member)
    earlier = dot_nn(member_hot, hot(new < old))
    rank = jnp.sum(jnp.where(member, earlier, 0.0), axis=0, keepdims=True)
    seg[0:1, :] = owner
    seg[1:2, :] = rank
    seg[2:8, :] = jnp.zeros((6, SEGS), F32)
    ranked = rank == iota((ND, SEGS), 0).astype(F32)
    table = 4.0 * dot_nt(member_hot, jnp.where(ranked, by_side[1:2], 0.0).astype(BF16))
    table = table + dot_nt(member_hot, jnp.where(ranked, by_side[2:3], 0.0).astype(BF16))
    code_out[...] = table.reshape(ND, 1, 128)

    for copy in loads[0]:
        copy.wait()
    face_rows(rs, NODES - 1, faces_r)
    pack_last(faces_r, last_out)
    for copy in loads[1]:
        copy.wait()
    face_rows(ss, 0, faces_s)
    make_table(faces_s, sproj_ref, tab, None)

    pl.semaphore_wait(barrier, ND - 1)

    block = lambda ref, i: ref.at[pl.ds(pl.multiple_of(i * BAND, 16), BAND), pl.ds(0, 256)]
    tail_block = lambda ref, i: ref.at[pl.ds(pl.multiple_of(i * BAND // 2, 8), BAND // 2)]

    def ring_send(i, src, dst, src_last, dst_last, sems):
        for n, (cut, a, b) in enumerate(((block, src, dst), (tail_block, src_last, dst_last))):
            pltpu.make_async_remote_copy(
                src_ref=cut(a, i), dst_ref=cut(b, mi),
                send_sem=sems.at[0, n], recv_sem=sems.at[1, n],
                device_id=(i, mj), device_id_type=MESH,
            ).start()

    def ring_wait(dst, dst_last, sems, side):
        rows = dst.at[pl.ds(0, (NR - 1) * BAND), pl.ds(0, 256)]
        pltpu.make_async_copy(rows, rows, sems.at[side, 0]).wait()
        rows = dst_last.at[pl.ds(0, (NR - 1) * BAND // 2)]
        pltpu.make_async_copy(rows, rows, sems.at[side, 1]).wait()

    def ring_own(src, dst, src_last, dst_last, n):
        return [
            pltpu.make_async_copy(block(src, mi), block(dst, mi), own_sem.at[n]),
            pltpu.make_async_copy(tail_block(src_last, mi), tail_block(dst_last, mi), own_sem.at[n + 1]),
        ]

    def send_code(p, carry):
        i, j = peer(p)
        pltpu.make_async_remote_copy(
            src_ref=code_out.at[i * NS + j], dst_ref=code_in.at[me],
            send_sem=code_sem.at[0], recv_sem=code_sem.at[1],
            device_id=(i, j), device_id_type=MESH,
        ).start()
        return carry

    def send_trace(p, carry):
        ring_send(lax.rem(mi + p, NR), faces_r, bands, last_out, last_in, trace_sem)
        return carry

    for p in range(1, ND):
        send_code(p, 0)
    lax.fori_loop(1, NR, send_trace, 0)
    own = pltpu.make_async_copy(code_out.at[me], code_in.at[me], own_sem.at[0])
    own.start()
    own_trace = ring_own(faces_r, bands, last_out, last_in, 6)
    for copy in own_trace:
        copy.start()

    volume(rs, ru, prim, tmp, acc, range(2))

    own.wait()
    part = code_in.at[pl.ds(0, ND - 1)]
    pltpu.make_async_copy(part, part, code_sem.at[1]).wait()
    codes[...] = code_in[...].reshape(ND, 128)

    def send_chunk(chunk, src, dst, sems):
        def send(p, carry):
            i, j = peer(p)
            at = pl.ds(pl.multiple_of(chunk * CHUNK_ROWS + (i * NS + j) * MSG, MSG), SENT)
            to = pl.ds(pl.multiple_of(chunk * CHUNK_ROWS + me * MSG, MSG), SENT)
            pltpu.make_async_remote_copy(
                src_ref=src.at[at], dst_ref=dst.at[to],
                send_sem=send_sem, recv_sem=sems.at[chunk],
                device_id=(i, j), device_id_type=MESH,
            ).start()
            return carry

        lax.fori_loop(1, ND, send, 0)

    def wait_chunk(chunk, dst, sems):
        rows = dst.at[pl.ds(chunk * CHUNK_ROWS, (ND - 1) * SENT)]
        pltpu.make_async_copy(rows, rows, sems.at[chunk]).wait()

    def own_chunk(chunk, src, dst, sem):
        to = pl.ds(pl.multiple_of(chunk * CHUNK_ROWS + me * MSG, MSG), SENT)
        return pltpu.make_async_copy(src.at[to], dst.at[to], sem)

    for chunk in range(2):
        for r in range(PAIRS):
            slot = chunk * PAIRS + r
            column = codes[:, slot : slot + 1].astype(jnp.int32) - 1
            hots[r * ND : r * ND + ND, :] = hot(column == iota((ND, SEGS), 1))
        gather_chunk(chunk, hots, tab, rout)
        send_chunk(chunk, rout, rin, r_sem)
        own_chunk(chunk, rout, rin, own_sem.at[2 + chunk]).start()

    for copy in own_trace:
        copy.wait()
    ring_wait(bands, last_in, trace_sem, 1)
    unpack_last(last_in, bands)
    make_table(bands, rproj_ref, ltab, lside)
    for chunk in range(2):
        belongs = seg[0:1, :] == iota((ND, SEGS), 0).astype(F32)
        for r in range(PAIRS):
            slot = chunk * PAIRS + r
            hots[r * ND : r * ND + ND, :] = hot(
                jnp.logical_and(belongs, seg[1:2, :] == float(slot))
            )
        gather_chunk(chunk, hots, ltab, lout)
        send_chunk(chunk, lout, lin, l_sem)
        own_chunk(chunk, lout, lin, own_sem.at[4 + chunk]).start()

    columns = seg[...].T.astype(jnp.int32)
    code_rows = codes[...].T.astype(jnp.int32)
    for s in range(2):
        rows = slice(s * ELEMS, s * ELEMS + ELEMS)
        slot = columns[rows, 1:2] * ND + columns[rows, 0:1]
        for r in range(CAP):
            cols = slice(r * ND, r * ND + ND)
            seg_hots[rows, cols] = hot(slot == iota((ELEMS, ND), 1) + r * ND)
            line = code_rows[r : r + 1, :] - (1 + s * ELEMS)
            sum_hots[rows, cols] = hot(line == iota((ELEMS, ND), 0))
    volume(rs, ru, prim, tmp, acc, range(2, 3))
    volume(ss, su, prim, tmp, acc, range(3))

    lower = iota((ND, 128), 1) < FACE
    for chunk in range(2):
        own_chunk(chunk, rout, rin, own_sem.at[2 + chunk]).wait()
        wait_chunk(chunk, rin, r_sem)
        for r in range(PAIRS):
            at = pl.ds((chunk * PAIRS + r) * ND, ND)
            for t in range(2):
                put_parts(arrived, at, t, rin[message_row(chunk, 2 * r + t), :])
            x = rin[message_row(chunk, 12 + r // 2), :]
            if r % 2:
                x = pltpu.roll(x, FACE, 1)
            put_parts(arrived, at, 2, jnp.where(lower, x, 0.0))
    for s in range(2):
        rows = slice(s * ELEMS, s * ELEMS + ELEMS)
        y, z = pick(seg_hots[rows, :], arrived)
        rside[rows, 0:256] = y
        rside[rows, 256:384] = z
    zero = jnp.zeros((FACE, FACE), F32)
    back = []
    for half in range(2):
        blocks = [
            jnp.concatenate([rproj_ref[s], zero] if half == 0 else [zero, rproj_ref[s]], axis=1)
            for s in range(2)
        ]
        back.append(split(jnp.concatenate(blocks, axis=0)))

    def band_flux(g, carry):
        rows = pl.ds(pl.multiple_of(g * 128, 128), 128)
        others = pl.ds(pl.multiple_of(ELEMS + g * 128, 128), 128)
        left = [lside[rows, v * 128 : v * 128 + 128] for v in range(5)]
        right = []
        for t in range(3):
            cols = slice(t * 128, t * 128 + 128)
            right += list(pair(rside[rows, cols], rside[others, cols]))
        flux = [split(x) for x in rusanov(left, right[:5])]
        for t in range(3):
            y = dot3(dot_nn, flux[2 * t], back[0])
            if t < 2:
                y = y + dot3(dot_nn, flux[2 * t + 1], back[1])
            rflux[rows, t * 128 : t * 128 + 128] = y
        return carry

    lax.fori_loop(0, 3, band_flux, 0)
    ring_wait(faces_r, last_out, trace_sem, 0)
    pack_last(rflux, last_out)

    def send_back(p, carry):
        ring_send(lax.rem(mi + p, NR), rflux, rflux_in, last_out, last_back, back_sem)
        return carry

    lax.fori_loop(1, NR, send_back, 0)
    own_back = ring_own(rflux, rflux_in, last_out, last_back, 8)
    for copy in own_back:
        copy.start()

    def fields(ref, chunk, pp):
        tile = lambda r, t: ref[message_row(chunk, 2 * (2 * pp + r) + t), :]
        return [
            *pair(tile(0, 0), tile(1, 0)),
            *pair(tile(0, 1), tile(1, 1)),
            ref[message_row(chunk, 12 + pp), :],
        ]

    for chunk in range(2):
        own_chunk(chunk, lout, lin, own_sem.at[4 + chunk]).wait()
        wait_chunk(chunk, lin, l_sem)
        for pp in range(HALF):
            slot = chunk * PAIRS + 2 * pp
            named = jnp.where(lower, codes[:, slot : slot + 1], codes[:, slot + 1 : slot + 2])
            flux = [
                jnp.where(named > 0.5, x, 0.0)
                for x in rusanov(fields(lin, chunk, pp), fields(rout, chunk, pp))
            ]
            first = [*pair(flux[0], flux[1])], [*pair(flux[2], flux[3])]
            last = (
                jnp.where(lower, flux[4], 0.0),
                jnp.where(lower, pltpu.roll(flux[4], FACE, 1), 0.0),
            )
            for r in range(2):
                at = pl.ds((2 * pp + r) * ND, ND)
                put_parts(arrived, at, 0, first[0][r])
                put_parts(arrived, at, 1, first[1][r])
                put_parts(arrived, at, 2, last[r])
        for s in range(2):
            rows = slice(s * ELEMS, s * ELEMS + ELEMS)
            some = sum_hots[rows, chunk * PAIRS * ND : (chunk + 1) * PAIRS * ND]
            y, z = pick(some, arrived.at[pl.ds(0, PAIRS * ND)])
            if chunk == 0:
                sums[rows, 0:256] = y
                sums[rows, 256:384] = z
            else:
                sums[rows, 0:256] += y
                sums[rows, 256:384] += z

    def face_flux(src, node):
        at = lambda v: pl.ds(v * 512 + node, FACE, stride=8)
        result = [[] for _ in range(5)]
        for g in range(3):
            fields = [src[g, at(v), :] for v in range(5)]
            u, p, _ = primitive(fields)
            for v, value in enumerate(flux_along(fields, u[2], p, 2)):
                result[v].append(value)
        return [jnp.concatenate(r, axis=1) for r in result]

    def add(out, node, v, change):
        for g in range(3):
            at = pl.ds(v * 512 + node, FACE, stride=8)
            out[g, at, :] = out[g, at, :] + change[:, g * 128 : g * 128 + 128]

    adjoint = jnp.concatenate([diagonal(sproj_ref[0]), diagonal(sproj_ref[1])], axis=0)
    adjoint = split(adjoint.T)
    mine = face_flux(ss, 0)
    for t in range(3):
        cols = slice(t * 128, t * 128 + 128)
        both = jnp.concatenate([sums[0:ELEMS, cols], sums[ELEMS : 2 * ELEMS, cols]], axis=1)
        y = dot3(dot_nt, adjoint, split(both))
        for vh in range(2 if t < 2 else 1):
            v = 2 * t + vh
            flux = 0.5 * y[vh * FACE : vh * FACE + FACE, :]
            add(su, 0, v, (TIME_STEP * LIFT) * (flux - mine[v]))

    mine = face_flux(rs, NODES - 1)
    for copy in own_back:
        copy.wait()
    ring_wait(rflux_in, last_back, back_sem, 1)
    unpack_last(last_back, rflux_in)
    for t in range(3):
        turned = jnp.concatenate(
            [rflux_in[g * 128 : g * 128 + 128, t * 128 : t * 128 + 128].T for g in range(3)], axis=1
        )
        for vh in range(2 if t < 2 else 1):
            v = 2 * t + vh
            y = turned[vh * FACE : vh * FACE + FACE, :]
            add(ru, NODES - 1, v, (-TIME_STEP * LIFT) * (0.5 * y - mine[v]))

    part = code_out.at[pl.ds(0, ND - 1)]
    pltpu.make_async_copy(part, part, code_sem.at[0]).wait()
    ring_wait(rflux, last_out, back_sem, 0)
    for chunk in range(4):
        rows = rout.at[pl.ds(0, (ND - 1) * SENT)]
        pltpu.make_async_copy(rows, rows, send_sem).wait()


def finish(ru, su, rnext, snext, sem):
    copies = [
        pltpu.make_async_copy(
            held.at[t, pl.ds(v * 512, 512)],
            out.at[pl.ds(v * 512, 512), pl.ds(t * 128, 128)],
            sem.at[n, t, v],
        )
        for n, (held, out) in enumerate(((ru, rnext), (su, snext)))
        for v in range(5)
        for t in range(3)
    ]
    for copy in copies:
        copy.start()
    for copy in copies:
        copy.wait()


def body(rotor_state, stator_state, rotor_projection, proj_stator, seg_owner, seg_row):
    vmem = pl.BlockSpec(memory_space=pltpu.VMEM)
    hbm = pl.BlockSpec(memory_space=pl.ANY)
    V = pltpu.VMEM
    dma = pltpu.SemaphoreType.DMA
    state = (ROWS, ELEMS)
    held = (3, ROWS, 128)
    big = jax.ShapeDtypeStruct(state, F32)
    parts = pl.pallas_call(
        mega,
        out_shape=(V(held, F32), V(held, F32)),
        in_specs=[vmem, vmem, vmem, vmem, hbm, hbm],
        scratch_shapes=[
            V(held, F32), V(held, F32),
            V((3 * 512, 128), F32), V((320, 128), F32), V((ROWS, 128), F32),
            V((ELEMS, 384), F32), V((ELEMS, 384), F32), V((ELEMS, 384), F32),
            V((ND, 1, 128), F32), V((ND, 1, 128), F32), V((ND, 128), F32), V((8, SEGS), F32),
            V((SEGS, SEGS), BF16), V((SEGS, SEGS), BF16), V((ELEMS, WIDE), F32), V((SEGS, 384), F32),
            V((PAIRS * ND, SEGS), BF16), V((SEGS, CAP * ND), BF16), V((SEGS, CAP * ND), BF16),
            V((2 * CHUNK_ROWS, 128), F32), V((2 * CHUNK_ROWS, 128), F32),
            V((2 * CHUNK_ROWS, 128), F32), V((2 * CHUNK_ROWS, 128), F32),
            V((ELEMS, 384), F32), V((ELEMS, 384), F32),
            V((ELEMS // 2, 128), F32), V((ELEMS // 2, 128), F32), V((ELEMS // 2, 128), F32),
            V((CAP * ND, SEGS), BF16), V((SEGS, 384), F32),
            dma((2, 3)), dma((10,)), dma((2,)), dma((2, 2)), dma, dma((2,)), dma((2,)), dma((2, 2)),
        ],
        compiler_params=pltpu.CompilerParams(
            collective_id=0, has_side_effects=True, vmem_limit_bytes=48 * 2**20
        ),
    )(
        seg_owner.reshape(1, SEGS),
        seg_row,
        rotor_projection,
        proj_stator,
        rotor_state.reshape(state),
        stator_state.reshape(state),
    )
    rotor_next, stator_next = pl.pallas_call(
        finish,
        out_shape=(big, big),
        in_specs=[hbm, hbm],
        out_specs=(hbm, hbm),
        scratch_shapes=[dma((2, 3, 5))],
        compiler_params=pltpu.CompilerParams(vmem_limit_bytes=4 * 2**20),
    )(*parts)
    return rotor_next.reshape(rotor_state.shape), stator_next.reshape(stator_state.shape)


def solution(mesh):
    spec = P(None, None, None, None, ("rotor", "stator"))
    in_specs = (spec, spec, P(), P(), P(("rotor", "stator"), None), P(("rotor", "stator")))
    return jax.shard_map(body, mesh=mesh, in_specs=in_specs, out_specs=(spec, spec), check_vma=False)
```

```python
import functools

import jax
import jax.numpy as jnp
import numpy as np
from jax import lax
from jax.experimental import pallas as pl
from jax.experimental.pallas import tpu as pltpu
from jax.sharding import PartitionSpec as P

NODES = 8
FACE = 64
NR = 8
NS = 16
ND = NR * NS
ELEMS = 384
BAND = ELEMS // NR
SEGS = 2 * ELEMS
ROWS = 5 * NODES * FACE
CAP = 12
PAIRS = CAP // 2
HALF = PAIRS // 2
MSG = 16
SENT = 15
CHUNK_ROWS = ND * MSG
WIDE = 5 * 128
GAMMA = 1.4
TIME_STEP = 0.02
LIFT = 28.0
MESH = pl.DeviceIdType.MESH
F32 = jnp.float32
BF16 = jnp.bfloat16


def cheb_matrix():
    degree = NODES - 1
    j = np.arange(degree + 1)
    points = -np.cos(np.pi * j / degree)
    weights = np.where((j == 0) | (j == degree), 2.0, 1.0) * (-1.0) ** j
    spacing = points[:, None] - points[None, :]
    identity = np.eye(degree + 1)
    matrix = weights[:, None] / weights[None, :] / (spacing + identity)
    matrix = matrix - identity * matrix.sum(axis=1)[:, None]
    return matrix.astype(np.float32)


DM = cheb_matrix().astype(np.float64) * (-TIME_STEP * 0.5)
ODD = DM[:4, :4] - DM[:4, :3:-1]
EVEN = DM[:4, :4] + DM[:4, :3:-1]


def derive(line):
    plus = [line[j] + line[7 - j] for j in range(4)]
    minus = [line[j] - line[7 - j] for j in range(4)]
    out = [None] * 8
    for i in range(4):
        p = sum(float(ODD[i, j]) * minus[j] for j in range(4))
        q = sum(float(EVEN[i, j]) * plus[j] for j in range(4))
        out[i] = p + q
        out[7 - i] = p - q
    return out


def primitive(fields):
    density, mx, my, mz, energy = fields
    inverse = 1.0 / density
    u = (mx * inverse, my * inverse, mz * inverse)
    kinetic = mx * u[0] + my * u[1] + mz * u[2]
    return u, (GAMMA - 1.0) * (energy - 0.5 * kinetic), inverse


def flux_along(fields, speed, pressure, direction):
    result = [fields[1 + direction]]
    for k in range(3):
        term = fields[1 + k] * speed
        result.append(term + pressure if k == direction else term)
    result.append((fields[4] + pressure) * speed)
    return result


def rusanov(left, right):
    lu, lp, li = primitive(left)
    ru, rp, ri = primitive(right)
    lf = flux_along(left, lu[2], lp, 2)
    rf = flux_along(right, ru[2], rp, 2)
    signal = jnp.maximum(
        jnp.abs(lu[2]) + jnp.sqrt(GAMMA * lp * li), jnp.abs(ru[2]) + jnp.sqrt(GAMMA * rp * ri)
    )
    return [
        0.5 * (lf[v] + rf[v]) - 0.5 * signal * (right[v] - left[v]) for v in range(5)
    ]


def split(x):
    hi = x.astype(BF16)
    return hi, (x - hi.astype(F32)).astype(BF16)


def dot_nn(a, b):
    return lax.dot_general(a, b, (((1,), (0,)), ((), ())), preferred_element_type=F32)


def dot_nt(a, b):
    return lax.dot_general(a, b, (((1,), (1,)), ((), ())), preferred_element_type=F32)


def dot3(dot, a, b):
    return dot(a[0], b[0]) + dot(a[0], b[1]) + dot(a[1], b[0])


def hot(mask):
    return jnp.where(mask, 1.0, 0.0).astype(BF16)


def iota(shape, dim):
    return lax.broadcasted_iota(jnp.int32, shape, dim)


def volume_first(src, prim, tmp, acc, step):
    t, a = lax.div(step, 8), lax.rem(step, 8)
    at = lambda v, b: pl.ds(pl.multiple_of(v * 512 + a * 64 + b * 8, 8), 8)
    lines = [[] for _ in range(5)]
    for b in range(8):
        fields = [src[t, at(v, b), :] for v in range(5)]
        u, p, _ = primitive(fields)
        prim[at(0, b), :] = u[0]
        prim[at(1, b), :] = u[2]
        prim[at(2, b), :] = p
        for v, value in enumerate(flux_along(fields, u[1], p, 1)):
            lines[v].append(value)
    for v in range(5):
        for b, value in enumerate(derive(lines[v])):
            acc[at(v, b), :] = value
    column = lambda v, c: pl.ds(v * 512 + a * 64 + c, 8, stride=8)
    lines = [[] for _ in range(5)]
    for c in range(8):
        fields = [None] + [src[t, column(v, c), :] for v in range(1, 5)]
        for v, value in enumerate(
            flux_along(fields, prim[column(1, c), :], prim[column(2, c), :], 2)
        ):
            lines[v].append(value)
    for v in range(5):
        for c, value in enumerate(derive(lines[v])):
            tmp[pl.ds(v * 64 + c, 8, stride=8), :] = value
    for v in range(5):
        for b in range(8):
            acc[at(v, b), :] += tmp[v * 64 + b * 8 : v * 64 + b * 8 + 8, :]


def volume_second(src, prim, acc, out, t, b):
    at = lambda v, a: pl.ds(pl.multiple_of(v * 512 + a * 64 + b * 8, 8), 8)
    lines = [[] for _ in range(5)]
    for a in range(8):
        fields = [None] + [src[t, at(v, a), :] for v in range(1, 5)]
        for v, value in enumerate(
            flux_along(fields, prim[at(0, a), :], prim[at(2, a), :], 0)
        ):
            lines[v].append(value)
    for v in range(5):
        for a, value in enumerate(derive(lines[v])):
            out[t, at(v, a), :] = src[t, at(v, a), :] + (acc[at(v, a), :] + value)


def volume(src, out, prim, tmp, acc, tiles):
    for t in tiles:

        def first(a, carry):
            volume_first(src, prim, tmp, acc, t * 8 + a)
            return carry

        def second(b, carry):
            volume_second(src, prim, acc, out, t, b)
            return carry

        lax.fori_loop(0, 8, first, 0)
        lax.fori_loop(0, 8, second, 0)


def face_rows(src, node, dst):
    for t in range(3):
        count = 128 if t < 2 else 64
        rows = [
            src[g, pl.ds(t * 1024 + node, count, stride=8), :]
            for g in range(3)
        ]
        for g in range(3):
            block = rows[g]
            if t == 2:
                block = jnp.concatenate([block, jnp.zeros((64, 128), F32)], axis=0)
            dst[g * 128 : g * 128 + 128, t * 128 : t * 128 + 128] = block.T


def pair(a, b):
    lower = iota(a.shape, 1) < FACE
    return (
        jnp.where(lower, a, pltpu.roll(b, FACE, 1)),
        jnp.where(lower, pltpu.roll(a, FACE, 1), b),
    )


def diagonal(matrix):
    zero = jnp.zeros((FACE, FACE), F32)
    top = jnp.concatenate([matrix, zero], axis=1)
    bottom = jnp.concatenate([zero, matrix], axis=1)
    return jnp.concatenate([top, bottom], axis=0)


def lanes_of(t):
    return (t * 128, 256 + t * 128) if t < 2 else (512, 640)


def put_parts(ref, rows, t, x):
    for start, piece in zip(lanes_of(t), split(x)):
        ref[rows, start : start + 128] = piece


def pick(hots, table):
    y = dot_nn(hots, table[:, 0:256]) + dot_nn(hots, table[:, 256:512])
    z = dot_nn(hots, table[:, 512:768])
    return y, z[:, :128] + z[:, 128:]


def make_table(faces, proj, table, side_ref):
    hi, lo = split(jnp.concatenate([diagonal(proj[0]), diagonal(proj[1])], axis=0))
    both = jnp.concatenate([hi, lo], axis=1)

    def body(g, carry):
        rows = pl.ds(pl.multiple_of(g * 128, 128), 128)
        for t in range(3):
            x, rest = split(faces[rows, t * 128 : t * 128 + 128])
            y = dot_nt(jnp.concatenate([x, x], axis=1), both) + dot_nt(rest, hi)
            sides = (y[:, :128], y[:, 128:])
            for s in range(2):
                at = pl.ds(pl.multiple_of(s * ELEMS + g * 128, 128), 128)
                put_parts(table, at, t, sides[s])
            if side_ref is not None:
                first, second = pair(*sides)
                side_ref[rows, 2 * t * 128 : 2 * t * 128 + 128] = first
                if t < 2:
                    side_ref[rows, 2 * t * 128 + 128 : 2 * t * 128 + 256] = second
        return carry

    lax.fori_loop(0, 3, body, 0)


def pack_last(faces, packed):
    lower = iota((BAND // 2, 128), 1) < FACE
    for i in range(NR):
        first = faces[i * BAND : i * BAND + BAND // 2, 256:384]
        second = faces[i * BAND + BAND // 2 : i * BAND + BAND, 256:384]
        packed[i * BAND // 2 : (i + 1) * BAND // 2, :] = jnp.where(
            lower, first, pltpu.roll(second, FACE, 1)
        )


def unpack_last(packed, faces):
    lower = iota((BAND // 2, 128), 1) < FACE
    for i in range(NR):
        x = packed[i * BAND // 2 : (i + 1) * BAND // 2, :]
        faces[i * BAND : i * BAND + BAND // 2, 256:384] = jnp.where(lower, x, 0.0)
        faces[i * BAND + BAND // 2 : i * BAND + BAND, 256:384] = jnp.where(
            lower, pltpu.roll(x, FACE, 1), 0.0
        )


def message_row(chunk, row):
    return pl.ds(chunk * CHUNK_ROWS + row, ND, stride=MSG)


def gather_chunk(chunk, hots, table, message):
    y, z = pick(hots[...], table)
    lower = iota((ND, 128), 1) < FACE
    for r in range(PAIRS):
        rows = slice(r * ND, r * ND + ND)
        for t in range(2):
            message[message_row(chunk, 2 * r + t), :] = y[rows, t * 128 : t * 128 + 128]
    for pp in range(HALF):
        even = z[2 * pp * ND : 2 * pp * ND + ND, :]
        odd = z[2 * pp * ND + ND : 2 * pp * ND + 2 * ND, :]
        message[message_row(chunk, 12 + pp), :] = jnp.where(lower, even, pltpu.roll(odd, FACE, 1))


def mega(
    owner_ref, row_ref, rproj_ref, sproj_ref, rstate, sstate,
    ru, su,
    rs, ss, prim, tmp, acc,
    faces_s, faces_r, bands, code_out, code_in, codes, seg,
    tab, ltab, lside, rside, hots, seg_hots, sum_hots,
    rout, rin, lout, lin, rflux, rflux_in, last_out, last_in, last_back, arrived, sums,
    load_sem, own_sem, code_sem, trace_sem, send_sem, r_sem, l_sem, back_sem,
):
    mi, mj = lax.axis_index("rotor"), lax.axis_index("stator")
    me = mi * NS + mj
    tiles = lambda ref, t: ref.at[:, pl.ds(t * 128, 128)]
    loads = [
        [
            pltpu.make_async_copy(tiles(state, t), held.at[t], load_sem.at[n, t])
            for t in range(3)
        ]
        for n, (state, held) in enumerate(((rstate, rs), (sstate, ss)))
    ]
    for copy in loads[0] + loads[1]:
        copy.start()

    def coords(d):
        return (lax.div(d, NS), lax.rem(d, NS))

    def peer(p):
        o = lax.rem(p * 53, ND)
        return lax.rem(lax.div(o, NS) + mi, NR), lax.rem(lax.rem(o, NS) + mj, NS)

    barrier = pltpu.get_barrier_semaphore()

    def greet(p, carry):
        pl.semaphore_signal(
            barrier, inc=1, device_id=coords(lax.rem(me + p, ND)), device_id_type=MESH
        )
        return carry

    lax.fori_loop(1, ND, greet, 0)

    owner = owner_ref[...].astype(F32)
    code = row_ref[...].reshape(1, SEGS)
    lane = iota((1, SEGS), 1)
    side = lax.rem(lane, 2)
    code = code + side * ELEMS + 1
    high = lax.div(code, 4).astype(F32)
    low = lax.rem(code, 4).astype(F32)
    packed = jnp.concatenate([owner, high, low, jnp.zeros((5, SEGS), F32)], axis=0).astype(BF16)
    new = iota((SEGS, SEGS), 0)
    old = iota((SEGS, SEGS), 1)
    order = hot(old == jnp.where(new < ELEMS, 2 * new, 2 * new - 2 * ELEMS + 1))
    by_side = dot_nt(packed, order)
    owner = by_side[0:1]
    member = owner == iota((ND, SEGS), 0).astype(F32)
    member_hot = hot(member)
    earlier = dot_nn(member_hot, hot(new < old))
    rank = jnp.sum(jnp.where(member, earlier, 0.0), axis=0, keepdims=True)
    seg[0:1, :] = owner
    seg[1:2, :] = rank
    seg[2:8, :] = jnp.zeros((6, SEGS), F32)
    ranked = rank == iota((ND, SEGS), 0).astype(F32)
    table = 4.0 * dot_nt(member_hot, jnp.where(ranked, by_side[1:2], 0.0).astype(BF16))
    table = table + dot_nt(member_hot, jnp.where(ranked, by_side[2:3], 0.0).astype(BF16))
    code_out[...] = table.reshape(ND, 1, 128)

    for copy in loads[0]:
        copy.wait()
    face_rows(rs, NODES - 1, faces_r)
    pack_last(faces_r, last_out)
    for copy in loads[1]:
        copy.wait()
    face_rows(ss, 0, faces_s)
    make_table(faces_s, sproj_ref, tab, None)

    pl.semaphore_wait(barrier, ND - 1)

    block = lambda ref, i: ref.at[pl.ds(pl.multiple_of(i * BAND, 16), BAND), pl.ds(0, 256)]
    tail_block = lambda ref, i: ref.at[pl.ds(pl.multiple_of(i * BAND // 2, 8), BAND // 2)]

    def ring_send(i, src, dst, src_last, dst_last, sems):
        for n, (cut, a, b) in enumerate(((block, src, dst), (tail_block, src_last, dst_last))):
            pltpu.make_async_remote_copy(
                src_ref=cut(a, i), dst_ref=cut(b, mi),
                send_sem=sems.at[0, n], recv_sem=sems.at[1, n],
                device_id=(i, mj), device_id_type=MESH,
            ).start()

    def ring_wait(dst, dst_last, sems, side):
        rows = dst.at[pl.ds(0, (NR - 1) * BAND), pl.ds(0, 256)]
        pltpu.make_async_copy(rows, rows, sems.at[side, 0]).wait()
        rows = dst_last.at[pl.ds(0, (NR - 1) * BAND // 2)]
        pltpu.make_async_copy(rows, rows, sems.at[side, 1]).wait()

    def ring_own(src, dst, src_last, dst_last, n):
        return [
            pltpu.make_async_copy(block(src, mi), block(dst, mi), own_sem.at[n]),
            pltpu.make_async_copy(tail_block(src_last, mi), tail_block(dst_last, mi), own_sem.at[n + 1]),
        ]

    def send_code(p, carry):
        i, j = peer(p)
        pltpu.make_async_remote_copy(
            src_ref=code_out.at[i * NS + j], dst_ref=code_in.at[me],
            send_sem=code_sem.at[0], recv_sem=code_sem.at[1],
            device_id=(i, j), device_id_type=MESH,
        ).start()
        return carry

    def send_trace(p, carry):
        ring_send(lax.rem(mi + p, NR), faces_r, bands, last_out, last_in, trace_sem)
        return carry

    for p in range(1, ND):
        send_code(p, 0)
    lax.fori_loop(1, NR, send_trace, 0)
    own = pltpu.make_async_copy(code_out.at[me], code_in.at[me], own_sem.at[0])
    own.start()
    own_trace = ring_own(faces_r, bands, last_out, last_in, 6)
    for copy in own_trace:
        copy.start()

    volume(rs, ru, prim, tmp, acc, range(1))

    own.wait()
    part = code_in.at[pl.ds(0, ND - 1)]
    pltpu.make_async_copy(part, part, code_sem.at[1]).wait()
    codes[...] = code_in[...].reshape(ND, 128)

    def send_chunk(chunk, src, dst, sems):
        def send(p, carry):
            i, j = peer(p)
            at = pl.ds(pl.multiple_of(chunk * CHUNK_ROWS + (i * NS + j) * MSG, MSG), SENT)
            to = pl.ds(pl.multiple_of(chunk * CHUNK_ROWS + me * MSG, MSG), SENT)
            pltpu.make_async_remote_copy(
                src_ref=src.at[at], dst_ref=dst.at[to],
                send_sem=send_sem, recv_sem=sems.at[chunk],
                device_id=(i, j), device_id_type=MESH,
            ).start()
            return carry

        lax.fori_loop(1, ND, send, 0)

    def wait_chunk(chunk, dst, sems):
        rows = dst.at[pl.ds(chunk * CHUNK_ROWS, (ND - 1) * SENT)]
        pltpu.make_async_copy(rows, rows, sems.at[chunk]).wait()

    def own_chunk(chunk, src, dst, sem):
        to = pl.ds(pl.multiple_of(chunk * CHUNK_ROWS + me * MSG, MSG), SENT)
        return pltpu.make_async_copy(src.at[to], dst.at[to], sem)

    for chunk in range(2):
        for r in range(PAIRS):
            slot = chunk * PAIRS + r
            column = codes[:, slot : slot + 1].astype(jnp.int32) - 1
            hots[r * ND : r * ND + ND, :] = hot(column == iota((ND, SEGS), 1))
        gather_chunk(chunk, hots, tab, rout)
        send_chunk(chunk, rout, rin, r_sem)
        own_chunk(chunk, rout, rin, own_sem.at[2 + chunk]).start()

    for copy in own_trace:
        copy.wait()
    ring_wait(bands, last_in, trace_sem, 1)
    unpack_last(last_in, bands)
    make_table(bands, rproj_ref, ltab, lside)
    for chunk in range(2):
        belongs = seg[0:1, :] == iota((ND, SEGS), 0).astype(F32)
        for r in range(PAIRS):
            slot = chunk * PAIRS + r
            hots[r * ND : r * ND + ND, :] = hot(
                jnp.logical_and(belongs, seg[1:2, :] == float(slot))
            )
        gather_chunk(chunk, hots, ltab, lout)
        send_chunk(chunk, lout, lin, l_sem)
        own_chunk(chunk, lout, lin, own_sem.at[4 + chunk]).start()

    columns = seg[...].T.astype(jnp.int32)
    code_rows = codes[...].T.astype(jnp.int32)
    for s in range(2):
        rows = slice(s * ELEMS, s * ELEMS + ELEMS)
        slot = columns[rows, 1:2] * ND + columns[rows, 0:1]
        for r in range(CAP):
            cols = slice(r * ND, r * ND + ND)
            seg_hots[rows, cols] = hot(slot == iota((ELEMS, ND), 1) + r * ND)
            line = code_rows[r : r + 1, :] - (1 + s * ELEMS)
            sum_hots[rows, cols] = hot(line == iota((ELEMS, ND), 0))
    volume(rs, ru, prim, tmp, acc, range(1, 3))
    volume(ss, su, prim, tmp, acc, range(3))

    lower = iota((ND, 128), 1) < FACE
    for chunk in range(2):
        own_chunk(chunk, rout, rin, own_sem.at[2 + chunk]).wait()
        wait_chunk(chunk, rin, r_sem)
        for r in range(PAIRS):
            at = pl.ds((chunk * PAIRS + r) * ND, ND)
            for t in range(2):
                put_parts(arrived, at, t, rin[message_row(chunk, 2 * r + t), :])
            x = rin[message_row(chunk, 12 + r // 2), :]
            if r % 2:
                x = pltpu.roll(x, FACE, 1)
            put_parts(arrived, at, 2, jnp.where(lower, x, 0.0))
    for s in range(2):
        rows = slice(s * ELEMS, s * ELEMS + ELEMS)
        y, z = pick(seg_hots[rows, :], arrived)
        rside[rows, 0:256] = y
        rside[rows, 256:384] = z
    zero = jnp.zeros((FACE, FACE), F32)
    back = []
    for half in range(2):
        blocks = [
            jnp.concatenate([rproj_ref[s], zero] if half == 0 else [zero, rproj_ref[s]], axis=1)
            for s in range(2)
        ]
        back.append(split(jnp.concatenate(blocks, axis=0)))

    def band_flux(g, carry):
        rows = pl.ds(pl.multiple_of(g * 128, 128), 128)
        others = pl.ds(pl.multiple_of(ELEMS + g * 128, 128), 128)
        left = [lside[rows, v * 128 : v * 128 + 128] for v in range(5)]
        right = []
        for t in range(3):
            cols = slice(t * 128, t * 128 + 128)
            right += list(pair(rside[rows, cols], rside[others, cols]))
        flux = [split(x) for x in rusanov(left, right[:5])]
        for t in range(3):
            y = dot3(dot_nn, flux[2 * t], back[0])
            if t < 2:
                y = y + dot3(dot_nn, flux[2 * t + 1], back[1])
            rflux[rows, t * 128 : t * 128 + 128] = y
        return carry

    lax.fori_loop(0, 3, band_flux, 0)
    ring_wait(faces_r, last_out, trace_sem, 0)
    pack_last(rflux, last_out)

    def send_back(p, carry):
        ring_send(lax.rem(mi + p, NR), rflux, rflux_in, last_out, last_back, back_sem)
        return carry

    lax.fori_loop(1, NR, send_back, 0)
    own_back = ring_own(rflux, rflux_in, last_out, last_back, 8)
    for copy in own_back:
        copy.start()

    def fields(ref, chunk, pp):
        tile = lambda r, t: ref[message_row(chunk, 2 * (2 * pp + r) + t), :]
        return [
            *pair(tile(0, 0), tile(1, 0)),
            *pair(tile(0, 1), tile(1, 1)),
            ref[message_row(chunk, 12 + pp), :],
        ]

    for chunk in range(2):
        own_chunk(chunk, lout, lin, own_sem.at[4 + chunk]).wait()
        wait_chunk(chunk, lin, l_sem)
        for pp in range(HALF):
            slot = chunk * PAIRS + 2 * pp
            named = jnp.where(lower, codes[:, slot : slot + 1], codes[:, slot + 1 : slot + 2])
            flux = [
                jnp.where(named > 0.5, x, 0.0)
                for x in rusanov(fields(lin, chunk, pp), fields(rout, chunk, pp))
            ]
            first = [*pair(flux[0], flux[1])], [*pair(flux[2], flux[3])]
            last = (
                jnp.where(lower, flux[4], 0.0),
                jnp.where(lower, pltpu.roll(flux[4], FACE, 1), 0.0),
            )
            for r in range(2):
                at = pl.ds((2 * pp + r) * ND, ND)
                put_parts(arrived, at, 0, first[0][r])
                put_parts(arrived, at, 1, first[1][r])
                put_parts(arrived, at, 2, last[r])
        for s in range(2):
            rows = slice(s * ELEMS, s * ELEMS + ELEMS)
            some = sum_hots[rows, chunk * PAIRS * ND : (chunk + 1) * PAIRS * ND]
            y, z = pick(some, arrived.at[pl.ds(0, PAIRS * ND)])
            if chunk == 0:
                sums[rows, 0:256] = y
                sums[rows, 256:384] = z
            else:
                sums[rows, 0:256] += y
                sums[rows, 256:384] += z

    def face_flux(src, node):
        at = lambda v: pl.ds(v * 512 + node, FACE, stride=8)
        result = [[] for _ in range(5)]
        for g in range(3):
            fields = [src[g, at(v), :] for v in range(5)]
            u, p, _ = primitive(fields)
            for v, value in enumerate(flux_along(fields, u[2], p, 2)):
                result[v].append(value)
        return [jnp.concatenate(r, axis=1) for r in result]

    def add(out, node, v, change):
        for g in range(3):
            at = pl.ds(v * 512 + node, FACE, stride=8)
            out[g, at, :] = out[g, at, :] + change[:, g * 128 : g * 128 + 128]

    adjoint = jnp.concatenate([diagonal(sproj_ref[0]), diagonal(sproj_ref[1])], axis=0)
    adjoint = split(adjoint.T)
    mine = face_flux(ss, 0)
    for t in range(3):
        cols = slice(t * 128, t * 128 + 128)
        both = jnp.concatenate([sums[0:ELEMS, cols], sums[ELEMS : 2 * ELEMS, cols]], axis=1)
        y = dot3(dot_nt, adjoint, split(both))
        for vh in range(2 if t < 2 else 1):
            v = 2 * t + vh
            flux = 0.5 * y[vh * FACE : vh * FACE + FACE, :]
            add(su, 0, v, (TIME_STEP * LIFT) * (flux - mine[v]))

    mine = face_flux(rs, NODES - 1)
    for copy in own_back:
        copy.wait()
    ring_wait(rflux_in, last_back, back_sem, 1)
    unpack_last(last_back, rflux_in)
    for t in range(3):
        turned = jnp.concatenate(
            [rflux_in[g * 128 : g * 128 + 128, t * 128 : t * 128 + 128].T for g in range(3)], axis=1
        )
        for vh in range(2 if t < 2 else 1):
            v = 2 * t + vh
            y = turned[vh * FACE : vh * FACE + FACE, :]
            add(ru, NODES - 1, v, (-TIME_STEP * LIFT) * (0.5 * y - mine[v]))

    part = code_out.at[pl.ds(0, ND - 1)]
    pltpu.make_async_copy(part, part, code_sem.at[0]).wait()
    ring_wait(rflux, last_out, back_sem, 0)
    for chunk in range(4):
        rows = rout.at[pl.ds(0, (ND - 1) * SENT)]
        pltpu.make_async_copy(rows, rows, send_sem).wait()


def finish(ru, su, rnext, snext, sem):
    copies = [
        pltpu.make_async_copy(
            held.at[t, pl.ds(v * 512, 512)],
            out.at[pl.ds(v * 512, 512), pl.ds(t * 128, 128)],
            sem.at[n, t, v],
        )
        for n, (held, out) in enumerate(((ru, rnext), (su, snext)))
        for v in range(5)
        for t in range(3)
    ]
    for copy in copies:
        copy.start()
    for copy in copies:
        copy.wait()


def body(rotor_state, stator_state, rotor_projection, proj_stator, seg_owner, seg_row):
    vmem = pl.BlockSpec(memory_space=pltpu.VMEM)
    hbm = pl.BlockSpec(memory_space=pl.ANY)
    V = pltpu.VMEM
    dma = pltpu.SemaphoreType.DMA
    state = (ROWS, ELEMS)
    held = (3, ROWS, 128)
    big = jax.ShapeDtypeStruct(state, F32)
    parts = pl.pallas_call(
        mega,
        out_shape=(V(held, F32), V(held, F32)),
        in_specs=[vmem, vmem, vmem, vmem, hbm, hbm],
        scratch_shapes=[
            V(held, F32), V(held, F32),
            V((3 * 512, 128), F32), V((320, 128), F32), V((ROWS, 128), F32),
            V((ELEMS, 384), F32), V((ELEMS, 384), F32), V((ELEMS, 384), F32),
            V((ND, 1, 128), F32), V((ND, 1, 128), F32), V((ND, 128), F32), V((8, SEGS), F32),
            V((SEGS, SEGS), BF16), V((SEGS, SEGS), BF16), V((ELEMS, WIDE), F32), V((SEGS, 384), F32),
            V((PAIRS * ND, SEGS), BF16), V((SEGS, CAP * ND), BF16), V((SEGS, CAP * ND), BF16),
            V((2 * CHUNK_ROWS, 128), F32), V((2 * CHUNK_ROWS, 128), F32),
            V((2 * CHUNK_ROWS, 128), F32), V((2 * CHUNK_ROWS, 128), F32),
            V((ELEMS, 384), F32), V((ELEMS, 384), F32),
            V((ELEMS // 2, 128), F32), V((ELEMS // 2, 128), F32), V((ELEMS // 2, 128), F32),
            V((CAP * ND, SEGS), BF16), V((SEGS, 384), F32),
            dma((2, 3)), dma((10,)), dma((2,)), dma((2, 2)), dma, dma((2,)), dma((2,)), dma((2, 2)),
        ],
        compiler_params=pltpu.CompilerParams(
            collective_id=0, has_side_effects=True, vmem_limit_bytes=48 * 2**20
        ),
    )(
        seg_owner.reshape(1, SEGS),
        seg_row,
        rotor_projection,
        proj_stator,
        rotor_state.reshape(state),
        stator_state.reshape(state),
    )
    rotor_next, stator_next = pl.pallas_call(
        finish,
        out_shape=(big, big),
        in_specs=[hbm, hbm],
        out_specs=(hbm, hbm),
        scratch_shapes=[dma((2, 3, 5))],
        compiler_params=pltpu.CompilerParams(vmem_limit_bytes=4 * 2**20),
    )(*parts)
    return rotor_next.reshape(rotor_state.shape), stator_next.reshape(stator_state.shape)


def solution(mesh):
    spec = P(None, None, None, None, ("rotor", "stator"))
    in_specs = (spec, spec, P(), P(), P(("rotor", "stator"), None), P(("rotor", "stator")))
    return jax.shard_map(body, mesh=mesh, in_specs=in_specs, out_specs=(spec, spec), check_vma=False)
```
